128 devices in a mesh: row: 16 (over x, y_lo, core), col: 8 (over z, y_hi).
Axes of the slice: x: 4, y: 4 (y_hi: 2, y_lo: 2; y = y_hi * 2 + y_lo), z: 4, core: 2. Of those that a mesh axis runs over, the one named last changes fastest.
Arguments:
- features: float32 [8, 64, 128, 1280], P('col', 'row'), may hold values from -256 to 256
- timestep: int32 [8], P('col'), may hold values from 0 to 999
- w_time: float32 [320, 1280], replicated, may hold values from -0.3125 to 0.3125
- w_emb: float32 [1280, 1280], replicated, may hold values from -0.15625 to 0.15625
- b_emb: float32 [1280], replicated, may hold values from -4 to 4
- gn_gain: float32 [1280], replicated, may hold values from 0.5 to 1.5
- gn_bias: float32 [1280], replicated, may hold values from -3 to 3
- w_query: bfloat16 [1280, 640], P('col'), may hold values from -0.5 to 0.5
- w_key: bfloat16 [1280, 640], P('col'), may hold values from -0.5 to 0.5
- w_value: bfloat16 [1280, 640], P('col'), may hold values from -0.15625 to 0.15625
- w_out: bfloat16 [640, 1280], P(None, 'col'), may hold values from -0.25 to 0.25
Outputs:
- block_out: float32 [8, 64, 128, 1280], P('col', 'row')
The draws below stay inside these ranges and needn't reach their ends.
All inputs are finite; a program needn't handle non-finite values.
Results may differ from the reference program's by a relative error of at most 0.0035.
The reference program's roundings to bfloat16 on the way (of `normed`, `probs` and `attended`) count: a program that leaves them out, or rounds other values in their place, can miss the bound.
Values may be sent and summed in bfloat16 or wider, within the bound.
No kernel may reach another device: no remote copies, remote signals or barrier semaphores. Data moves between devices by JAX's collectives and lax.ppermute only.
A program may use at most 128 MiB of HBM per device.

```python
import math
import jax
import jax.numpy as jnp
from jax import lax

C = 1280
GROUPS = 32
HEADS = 10
HEAD = 64
TEMB = 320
COLS = 128
INNER = 640
IMAGES = 8
IMG_ROWS = 64
TOKENS = 8192


def shared_matrix(key):
    return jax.random.normal(key, (C, HEADS * HEAD), jnp.float32)


def mixed_projection(key, salt):
    common = shared_matrix(key)
    key = jax.random.fold_in(key, salt)
    own = jax.random.normal(key, (C, HEADS * HEAD), jnp.float32)
    mixed = (0.92 * own + 0.39 * common) * (1.73 / math.sqrt(C))
    return jnp.clip(mixed, -0.5, 0.5).astype(jnp.bfloat16)


def draw_w_query(key, part):
    return mixed_projection(key, 21)


def draw_w_key(key, part):
    return mixed_projection(key, 22)


def draw_features(key, part):
    key = jax.random.fold_in(key, 5)
    keys = jax.random.split(key, 3)
    shape = (IMAGES, IMG_ROWS, COLS, C)
    steps = jnp.arange(IMG_ROWS, dtype=jnp.float32) / max(IMG_ROWS - 1, 1)
    base = jnp.clip(jax.random.normal(keys[0], shape, jnp.float32), -4.0, 4.0)
    rising = 1.0 + 2.0 * steps
    channel = jnp.exp(jax.random.uniform(keys[1], (C,), jnp.float32, 0.0, math.log(10.0)))
    pixel = jax.random.uniform(keys[2], (IMAGES, IMG_ROWS, COLS, 1), jnp.float32, 0.5, 1.5)
    field = 0.25 * base * rising[None, :, None, None] * channel * pixel
    return jnp.clip(field, -256.0, 256.0)


def plant(values, own_key, smallest, high):
    extent = values.shape
    spot = [jax.random.randint(jax.random.fold_in(own_key, axis), (), 0, extent[axis]) for axis in range(len(extent))]
    values = values.at[tuple(spot)].set(smallest)
    longest = extent.index(max(extent))
    spot[longest] = (spot[longest] + 1) % extent[longest]
    return values.at[tuple(spot)].set(high)


def block_scale(key, extent, cuts, least, high):
    level, own = 1.0, jax.random.fold_in(key, 6)
    for position, blocks in cuts:
        heights = jnp.exp(jax.random.uniform(jax.random.fold_in(own, position), (blocks,), jnp.float32, least / len(cuts), high / len(cuts)))
        level = level * jnp.repeat(heights, extent[position] // blocks).reshape([-1 if axis == position else 1 for axis in range(len(extent))])
    return level


def scatter_about(own_key, shape, width, most, pieces=(), held_as=jnp.bfloat16):
    drawn = jax.random.normal(own_key, shape, jnp.float32) * width
    if len(pieces) > 0:
        drawn = block_scale(own_key, shape, pieces, -0.22, 0.18) * drawn
    return jnp.clip(drawn, min=-most, max=most).astype(held_as)


def setup_inputs(seed: int = 0) -> dict:
    key_list = jax.random.split(jax.random.key(seed), 12)
    return {
        "features": draw_features(jax.random.fold_in(key_list[11], 71), 0),
        "timestep": plant(jax.random.randint(key_list[1], (IMAGES,), 0, 1000), jax.random.fold_in(key_list[1], 1), 0, 999).astype(jnp.int32),
        "w_time": scatter_about(key_list[2], (TEMB, C), TEMB ** -0.5, 0.3125, (), jnp.float32),
        "w_emb": scatter_about(key_list[3], (C, C), C ** -0.5, 0.15625, (), jnp.float32),
        "b_emb": scatter_about(key_list[4], (C,), 1.0, 4.0, (), jnp.float32),
        "gn_gain": jnp.clip(1.0 + 0.1 * jax.random.normal(key_list[5], (C,), jnp.float32), 0.5, 1.5),
        "gn_bias": scatter_about(key_list[6], (C,), 0.5, 3.0, (), jnp.float32),
        "w_query": draw_w_query(jax.random.fold_in(key_list[11], 71), 0),
        "w_key": draw_w_key(jax.random.fold_in(key_list[11], 71), 0),
        "w_value": scatter_about(key_list[9], (C, INNER), C ** -0.5, 0.15625, ((0, 8),)),
        "w_out": scatter_about(key_list[10], (INNER, C), INNER ** -0.5, 0.25, ((1, 8),)),
    }


def time_shift(step_value, w_time, w_emb, b_emb):
    half = w_time.shape[0] // 2
    freqs = jnp.exp(-math.log(10000.0) * jnp.arange(half, dtype=jnp.float32) / half)
    angles = step_value.astype(jnp.float32) * freqs
    table = jnp.concatenate([jnp.cos(angles), jnp.sin(angles)])[None, :]
    hidden = jax.nn.silu(jnp.dot(table, w_time, precision=lax.Precision.HIGHEST))
    return jnp.dot(hidden, w_emb, precision=lax.Precision.HIGHEST) + b_emb[None, :]

def one_image(image, step_value, w_time, w_emb, b_emb, gn_gain, gn_bias, w_query, w_key, w_value, w_out):
    shift = time_shift(step_value, w_time, w_emb, b_emb)
    lifted = image.reshape(TOKENS, C) + shift
    grouped = lifted.reshape(TOKENS, GROUPS, C // GROUPS)
    mean = lax.optimization_barrier(jnp.mean(grouped, axis=(0, 2), keepdims=True))
    var = lax.optimization_barrier(jnp.mean((grouped - mean) ** 2, axis=(0, 2), keepdims=True))
    normed = ((grouped - mean) / jnp.sqrt(var + 1e-06)).reshape(TOKENS, C) * gn_gain + gn_bias
    normed = normed.astype(jnp.bfloat16)
    query = jnp.dot(normed, w_query, preferred_element_type=jnp.float32).astype(jnp.bfloat16)
    key = jnp.dot(normed, w_key, preferred_element_type=jnp.float32).astype(jnp.bfloat16)
    value = jnp.dot(normed, w_value, preferred_element_type=jnp.float32).astype(jnp.bfloat16)
    key3 = key.astype(jnp.float32).reshape(TOKENS, HEADS, HEAD)
    value3 = value.astype(jnp.float32).reshape(TOKENS, HEADS, HEAD)
    block = 512 if TOKENS % 512 == 0 else TOKENS
    query_blocks = query.astype(jnp.float32).reshape(TOKENS // block, block, HEADS, HEAD)
    scale = 1.0 / math.sqrt(HEAD)

    def one_block(query_block):
        scores = jnp.einsum('qhd,khd->hqk', query_block, key3, precision=lax.Precision.HIGHEST) * scale
        top = lax.optimization_barrier(jnp.max(scores, axis=-1, keepdims=True))
        weights = jnp.exp(scores - top)
        total = lax.optimization_barrier(jnp.sum(weights, axis=-1))
        probs = lax.optimization_barrier(weights.astype(jnp.bfloat16)).astype(jnp.float32)
        mixed = jnp.einsum('hqk,khd->qhd', probs, value3, precision=lax.Precision.HIGHEST)
        return (mixed / jnp.transpose(total)[:, :, None]).astype(jnp.bfloat16)
    attended = lax.map(one_block, query_blocks).reshape(TOKENS, HEADS * HEAD)
    block_out = lifted + jnp.dot(attended, w_out, preferred_element_type=jnp.float32)
    return block_out.reshape(IMG_ROWS, COLS, C)

def reference(features, timestep, w_time, w_emb, b_emb, gn_gain, gn_bias, w_query, w_key, w_value, w_out):
    outputs = []
    for index in range(IMAGES):
        outputs.append(one_image(features[index], timestep[index], w_time, w_emb, b_emb, gn_gain, gn_bias, w_query, w_key, w_value, w_out))
    return jnp.stack(outputs)
```

```python
import functools
import math

import jax
import jax.numpy as jnp
from jax import lax
from jax.experimental import pallas as pl
from jax.experimental.pallas import tpu as pltpu
from jax.sharding import PartitionSpec as P

GROUPS = 32
HEADS = 10
HEAD = 64
CHIPS = 8
F32 = jnp.float32
BF16 = jnp.bfloat16
SCALE = math.log2(math.e) / math.sqrt(HEAD)


def time_shift(step_value, w_time, w_emb, b_emb):
    half = w_time.shape[0] // 2
    freqs = jnp.exp(-math.log(10000.0) * jnp.arange(half, dtype=F32) / half)
    angles = step_value.astype(F32) * freqs
    table = jnp.concatenate([jnp.cos(angles), jnp.sin(angles)])[None, :]
    hidden = jax.nn.silu(jnp.dot(table, w_time, precision=lax.Precision.HIGHEST))
    return jnp.dot(hidden, w_emb, precision=lax.Precision.HIGHEST) + b_emb[None, :]


def move_row(value, target):
    return lax.ppermute(value, "row", [(r, target(r)) for r in range(16)])


def move_col(value, target):
    return lax.ppermute(value, "col", [(c, target(c)) for c in range(8)])


def along_x(step):
    return lambda r: ((r // 4 + step) % 4) * 4 + r % 4


def along_z(step):
    return lambda c: ((c // 2 + step) % 4) * 2 + c % 2


def other_core(value):
    return move_row(value, lambda r: r ^ 1)


def across_chips(value):
    groups = [list(range(0, 16, 2)), list(range(1, 16, 2))]
    return lax.all_to_all(value, "row", 0, 0, tiled=True, axis_index_groups=groups)


def pooled(parts, count):
    mean = sum(p[0] for p in parts) / len(parts)
    spread = sum(p[1] for p in parts) + count * sum((p[0] - mean) ** 2 for p in parts)
    return jnp.stack([mean, spread])


def pooled_over_row(stat, count):
    parts = [stat] + [move_row(stat, along_x(d)) for d in (1, 2, 3)]
    stat = pooled(parts, count)
    parts = [stat] + [move_row(stat, lambda r, k=k: r ^ k) for k in (1, 2, 3)]
    return pooled(parts, 4 * count)


def gathered_weights(w_query, w_key, w_value):
    core = lax.axis_index("row") % 2
    z = lax.axis_index("col") // 2
    y_hi = lax.axis_index("col") % 2
    half = w_key.shape[1] // 2
    first = jnp.concatenate([w_query, w_key[:, :half]], axis=1)
    second = jnp.concatenate([w_key[:, half:], w_value], axis=1)
    mine = jnp.where(core == 0, first, second)
    depth, width = mine.shape
    theirs = move_col(mine, lambda c: c ^ 1)
    slab = jnp.where(y_hi == 0, jnp.stack([mine, theirs]), jnp.stack([theirs, mine]))
    below = move_col(slab, along_z(1))
    above = move_col(slab, along_z(-1))
    far_0 = move_col(below[0], along_z(1))
    far_1 = move_col(above[1], along_z(-1))
    whole = jnp.zeros((2, 4, 2, depth, width), BF16)

    def put(whole, piece, where_z, where_y):
        at = (core, where_z % 4, where_y, 0, 0)
        whole = lax.dynamic_update_slice(whole, piece[None, None], at)
        at = (1 - core, where_z % 4, where_y, 0, 0)
        return lax.dynamic_update_slice(whole, other_core(piece)[None, None], at)

    whole = put(whole, slab, z, 0)
    whole = put(whole, below, z + 3, 0)
    whole = put(whole, above, z + 1, 0)
    whole = put(whole, far_0[None], z + 2, 0)
    whole = put(whole, far_1[None], z + 2, 1)
    return whole.reshape(2, 8 * depth, width)


def split3(value):
    high = value.astype(BF16)
    rest = value - high.astype(F32)
    middle = rest.astype(BF16)
    low = (rest - middle.astype(F32)).astype(BF16)
    return high, middle, low


def product(a, b):
    return lax.dot_general(a, b, (((1,), (0,)), ((), ())), preferred_element_type=F32)


def put_keys(keys, vals, place, key_t, value_t):
    count = key_t.shape[1]
    row = lax.broadcasted_iota(jnp.int32, (HEAD, count), 0)
    ones = jnp.where(row < 3, 1.0, 0.0).astype(BF16)
    wide = jnp.concatenate([key_t, key_t, key_t, ones], axis=0)
    keys[place : place + count, :] = wide.T
    vals[:, place : place + count] = value_t


def put_top(query, top):
    width = top.shape[1]
    row = lax.broadcasted_iota(jnp.int32, (HEAD, width), 0)
    high, middle, low = split3(-top)
    wide = [jnp.broadcast_to(part, (HEAD, width)).astype(F32) for part in (high, middle, low)]
    rows = jnp.where(row == 0, wide[0], jnp.where(row == 1, wide[1], jnp.where(row == 2, wide[2], 0.0)))
    query[3 * HEAD :, :] = rows.astype(BF16)


def attend_rows(query, keys, vals, total_ref, accum_ref, query_t, chunk):
    width = query_t.shape[1]
    count = keys.shape[0]
    for at, part in enumerate(split3(query_t.astype(F32) * SCALE)):
        query[at * HEAD : (at + 1) * HEAD, :] = part

    def scores(start, size):
        return product(keys[pl.ds(start, size), :], query[...])

    def run(top):
        put_top(query, top)

        def step(i, state):
            total, accum = state
            start = pl.multiple_of(i * chunk, chunk)
            weights = jnp.exp2(scores(start, chunk))
            total = total + jnp.sum(weights.reshape(chunk // 8, 8, width), axis=0)
            accum = accum + product(vals[:, pl.ds(start, chunk)], weights.astype(BF16))
            return total, accum

        state = (jnp.zeros((8, width), F32), jnp.zeros((HEAD, width), F32))
        total, accum = lax.fori_loop(0, count // chunk, step, state)
        total_ref[...] = jnp.sum(total, axis=0, keepdims=True)
        accum_ref[...] = accum

    query[3 * HEAD :, :] = jnp.zeros((HEAD, width), BF16)
    run(jnp.max(scores(0, 256), axis=0, keepdims=True))
    small = jnp.max(jnp.where(total_ref[...] < 1e30, 0.0, 1.0))

    @pl.when(small > 0.5)
    def _():
        query[3 * HEAD :, :] = jnp.zeros((HEAD, width), BF16)

        def step(i, top):
            start = pl.multiple_of(i * 512, 512)
            return jnp.maximum(top, jnp.max(scores(start, 512), axis=0, keepdims=True))

        run(lax.fori_loop(0, count // 512, step, jnp.full((1, width), -jnp.inf, F32)))

    return (accum_ref[...] / total_ref[...]).astype(BF16)


def attention_scratch(count, width):
    return [
        pltpu.VMEM((4 * HEAD, width), BF16),
        pltpu.VMEM((count, 4 * HEAD), BF16),
        pltpu.VMEM((HEAD, count), BF16),
        pltpu.VMEM((1, width), F32),
        pltpu.VMEM((HEAD, width), F32),
    ]


def cost(queries, count):
    return pl.CostEstimate(
        flops=4 * queries * count * HEAD, bytes_accessed=8 * 1024 * 1024, transcendentals=queries * count
    )


def one_head_kernel(query_ref, mine_ref, theirs_ref, out_ref, *scratch):
    query, keys, vals, total, accum = scratch
    sources, unused, pixels = mine_ref.shape
    per_step = query_ref.shape[0]

    @pl.when(pl.program_id(0) == 0)
    def _():
        for s in range(sources):
            put_keys(keys, vals, s * pixels, mine_ref[s, HEAD : 2 * HEAD], mine_ref[s, 2 * HEAD :])
            put_keys(keys, vals, (sources + s) * pixels, theirs_ref[s, :HEAD], theirs_ref[s, HEAD:])

    query_t = jnp.concatenate([query_ref[s] for s in range(per_step)], axis=1)
    attended = attend_rows(query, keys, vals, total, accum, query_t, 1024)
    for s in range(per_step):
        out_ref[s] = attended[:, s * pixels : (s + 1) * pixels]


def one_head(mine, theirs):
    sources, unused, pixels = mine.shape
    per_step = 2
    count = 2 * sources * pixels
    return pl.pallas_call(
        one_head_kernel,
        grid=(sources // per_step,),
        in_specs=[
            pl.BlockSpec((per_step, HEAD, pixels), lambda i: (i, 0, 0)),
            pl.BlockSpec(mine.shape, lambda i: (0, 0, 0)),
            pl.BlockSpec(theirs.shape, lambda i: (0, 0, 0)),
        ],
        out_specs=pl.BlockSpec((per_step, HEAD, pixels), lambda i: (i, 0, 0)),
        out_shape=jax.ShapeDtypeStruct((sources, HEAD, pixels), BF16),
        scratch_shapes=attention_scratch(count, per_step * pixels),
        compiler_params=pltpu.CompilerParams(vmem_limit_bytes=56 * 2**20),
        cost_estimate=cost(sources * pixels, count),
    )(mine, mine, theirs)


def own_rows_kernel(query_ref, key_ref, value_ref, out_ref, *scratch):
    query, keys, vals, total, accum = scratch
    sources, unused, pixels = key_ref.shape
    for s in range(sources):
        put_keys(keys, vals, s * pixels, key_ref[s], value_ref[s])
    out_ref[...] = attend_rows(query, keys, vals, total, accum, query_ref[...], 2048)


def own_rows(query_t, pairs):
    heads = query_t.shape[0] // HEAD
    sources, unused, pixels = pairs.shape
    count = sources * pixels
    return pl.pallas_call(
        own_rows_kernel,
        grid=(heads,),
        in_specs=[
            pl.BlockSpec((HEAD, pixels), lambda h: (h, 0)),
            pl.BlockSpec((sources, HEAD, pixels), lambda h: (0, h, 0)),
            pl.BlockSpec((sources, HEAD, pixels), lambda h: (0, heads + h, 0)),
        ],
        out_specs=pl.BlockSpec((HEAD, pixels), lambda h: (h, 0)),
        out_shape=jax.ShapeDtypeStruct(query_t.shape, BF16),
        scratch_shapes=attention_scratch(count, pixels),
        compiler_params=pltpu.CompilerParams(vmem_limit_bytes=56 * 2**20),
        cost_estimate=cost(heads * pixels, count),
    )(query_t, pairs, pairs)


def local(
    features, timestep, w_time, w_emb, b_emb, gn_gain, gn_bias, w_query, w_key, w_value, w_out
):
    unused_one, rows_here, cols_here, channels = features.shape
    pixels = rows_here * cols_here
    per_group = channels // GROUPS
    inner = HEADS * HEAD
    weights = gathered_weights(w_query, w_key, w_value)
    full_out = lax.all_gather(w_out, "col", axis=1, tiled=True)

    shift = time_shift(timestep[0], w_time, w_emb, b_emb)
    lifted = features.reshape(pixels, channels) + shift
    count = float(pixels * per_group)

    def by_group(value):
        return jnp.sum(jnp.sum(value, axis=0).reshape(GROUPS, per_group), axis=1)

    def by_channel(value):
        return jnp.repeat(value, per_group)[None, :]

    mean_here = by_group(lifted) / count
    spread_here = by_group((lifted - by_channel(mean_here)) ** 2)
    mean, spread = pooled_over_row(jnp.stack([mean_here, spread_here]), count)
    var = spread / (count * lax.axis_size("row"))
    normed = (lifted - by_channel(mean)) / by_channel(jnp.sqrt(var + 1e-06)) * gn_gain + gn_bias
    normed = normed.astype(BF16)

    rows = lax.dot_general(weights, normed, (((1,), (1,)), ((), ())), preferred_element_type=F32)
    rows = rows.astype(BF16).reshape(3, inner, pixels)
    first = CHIPS * HEAD
    by_head = rows[:, :first].reshape(3, CHIPS, HEAD, pixels).transpose(1, 0, 2, 3)
    mine = across_chips(by_head.reshape(CHIPS, 3 * HEAD, pixels))
    theirs = other_core(mine[:, HEAD:])
    pairs, mine = lax.optimization_barrier((rows[1:, first:], mine))
    pairs = lax.all_gather(pairs.reshape(2 * (inner - first), pixels), "row", axis=0, tiled=False)
    attended = across_chips(one_head(mine, theirs)).reshape(first, pixels)
    others = own_rows(rows[0, first:], pairs)
    attended = jnp.concatenate([attended, others], axis=0)
    added = lax.dot_general(attended, full_out, (((0,), (0,)), ((), ())), preferred_element_type=F32)
    return (lifted + added).reshape(1, rows_here, cols_here, channels)


def solution(mesh):
    return jax.shard_map(
        local,
        mesh=mesh,
        in_specs=(
            P("col", "row", None, None),
            P("col"),
            P(),
            P(),
            P(),
            P(),
            P(),
            P("col", None),
            P("col", None),
            P("col", None),
            P(None, "col"),
        ),
        out_specs=P("col", "row", None, None),
        check_vma=False,
    )
```

```python
import functools
import math

import jax
import jax.numpy as jnp
from jax import lax
from jax.experimental import pallas as pl
from jax.experimental.pallas import tpu as pltpu
from jax.sharding import PartitionSpec as P

GROUPS = 32
HEADS = 10
HEAD = 64
CHIPS = 8
F32 = jnp.float32
BF16 = jnp.bfloat16
SCALE = math.log2(math.e) / math.sqrt(HEAD)


def time_shift(step_value, w_time, w_emb, b_emb):
    half = w_time.shape[0] // 2
    freqs = jnp.exp(-math.log(10000.0) * jnp.arange(half, dtype=F32) / half)
    angles = step_value.astype(F32) * freqs
    table = jnp.concatenate([jnp.cos(angles), jnp.sin(angles)])[None, :]
    hidden = jax.nn.silu(jnp.dot(table, w_time, precision=lax.Precision.HIGHEST))
    return jnp.dot(hidden, w_emb, precision=lax.Precision.HIGHEST) + b_emb[None, :]


def move_row(value, target):
    return lax.ppermute(value, "row", [(r, target(r)) for r in range(16)])


def move_col(value, target):
    return lax.ppermute(value, "col", [(c, target(c)) for c in range(8)])


def along_x(step):
    return lambda r: ((r // 4 + step) % 4) * 4 + r % 4


def along_z(step):
    return lambda c: ((c // 2 + step) % 4) * 2 + c % 2


def other_core(value):
    return move_row(value, lambda r: r ^ 1)


def across_chips(value):
    groups = [list(range(0, 16, 2)), list(range(1, 16, 2))]
    return lax.all_to_all(value, "row", 0, 0, tiled=True, axis_index_groups=groups)


def pooled(parts, count):
    mean = sum(p[0] for p in parts) / len(parts)
    spread = sum(p[1] for p in parts) + count * sum((p[0] - mean) ** 2 for p in parts)
    return jnp.stack([mean, spread])


def pooled_over_row(stat, count):
    parts = [stat] + [move_row(stat, along_x(d)) for d in (1, 2, 3)]
    stat = pooled(parts, count)
    parts = [stat] + [move_row(stat, lambda r, k=k: r ^ k) for k in (1, 2, 3)]
    return pooled(parts, 4 * count)


def half_weights(w_query, w_key, w_value):
    core = lax.axis_index("row") % 2
    half = w_key.shape[1] // 2
    first = jnp.concatenate([w_query, w_key[:, :half]], axis=1)
    second = jnp.concatenate([w_key[:, half:], w_value], axis=1)
    return jnp.where(core == 0, first, second)


def gathered_weights(mine, theirs):
    core = lax.axis_index("row") % 2
    z = lax.axis_index("col") // 2
    y_hi = lax.axis_index("col") % 2
    depth, width = mine.shape
    slab = jnp.where(y_hi == 0, jnp.stack([mine, theirs]), jnp.stack([theirs, mine]))
    below = move_col(slab, along_z(1))
    above = move_col(slab, along_z(-1))
    far_0 = move_col(below[0], along_z(1))
    far_1 = move_col(above[1], along_z(-1))
    whole = jnp.zeros((2, 4, 2, depth, width), BF16)

    def put(whole, piece, where_z, where_y):
        at = (core, where_z % 4, where_y, 0, 0)
        whole = lax.dynamic_update_slice(whole, piece[None, None], at)
        at = (1 - core, where_z % 4, where_y, 0, 0)
        return lax.dynamic_update_slice(whole, other_core(piece)[None, None], at)

    whole = put(whole, slab, z, 0)
    whole = put(whole, below, z + 3, 0)
    whole = put(whole, above, z + 1, 0)
    whole = put(whole, far_0[None], z + 2, 0)
    whole = put(whole, far_1[None], z + 2, 1)
    return whole.reshape(2, 8 * depth, width)


def split3(value):
    high = value.astype(BF16)
    rest = value - high.astype(F32)
    middle = rest.astype(BF16)
    low = (rest - middle.astype(F32)).astype(BF16)
    return high, middle, low


def product(a, b):
    return lax.dot_general(a, b, (((1,), (0,)), ((), ())), preferred_element_type=F32)


def put_keys(keys, vals, place, key_t, value_t):
    count = key_t.shape[1]
    row = lax.broadcasted_iota(jnp.int32, (HEAD, count), 0)
    ones = jnp.where(row < 3, 1.0, 0.0).astype(BF16)
    wide = jnp.concatenate([key_t, key_t, key_t, ones], axis=0)
    keys[place : place + count, :] = wide.T
    vals[:, place : place + count] = value_t


def put_top(query, top):
    width = top.shape[1]
    row = lax.broadcasted_iota(jnp.int32, (HEAD, width), 0)
    high, middle, low = split3(-top)
    wide = [jnp.broadcast_to(part, (HEAD, width)).astype(F32) for part in (high, middle, low)]
    rows = jnp.where(row == 0, wide[0], jnp.where(row == 1, wide[1], jnp.where(row == 2, wide[2], 0.0)))
    query[3 * HEAD :, :] = rows.astype(BF16)


def attend_rows(query, keys, vals, total_ref, accum_ref, query_t, chunk):
    width = query_t.shape[1]
    count = keys.shape[0]
    for at, part in enumerate(split3(query_t.astype(F32) * SCALE)):
        query[at * HEAD : (at + 1) * HEAD, :] = part

    def scores(start, size):
        return product(keys[pl.ds(start, size), :], query[...])

    def run(top):
        put_top(query, top)

        def step(i, state):
            total, accum = state
            start = pl.multiple_of(i * chunk, chunk)
            weights = jnp.exp2(scores(start, chunk))
            total = total + jnp.sum(weights.reshape(chunk // 8, 8, width), axis=0)
            accum = accum + product(vals[:, pl.ds(start, chunk)], weights.astype(BF16))
            return total, accum

        state = (jnp.zeros((8, width), F32), jnp.zeros((HEAD, width), F32))
        total, accum = lax.fori_loop(0, count // chunk, step, state)
        total_ref[...] = jnp.sum(total, axis=0, keepdims=True)
        accum_ref[...] = accum

    query[3 * HEAD :, :] = jnp.zeros((HEAD, width), BF16)
    run(jnp.max(scores(0, 256), axis=0, keepdims=True))
    small = jnp.max(jnp.where(total_ref[...] < 1e30, 0.0, 1.0))

    @pl.when(small > 0.5)
    def _():
        query[3 * HEAD :, :] = jnp.zeros((HEAD, width), BF16)

        def step(i, top):
            start = pl.multiple_of(i * 512, 512)
            return jnp.maximum(top, jnp.max(scores(start, 512), axis=0, keepdims=True))

        run(lax.fori_loop(0, count // 512, step, jnp.full((1, width), -jnp.inf, F32)))

    return (accum_ref[...] / total_ref[...]).astype(BF16)


def attention_scratch(count, width):
    return [
        pltpu.VMEM((4 * HEAD, width), BF16),
        pltpu.VMEM((count, 4 * HEAD), BF16),
        pltpu.VMEM((HEAD, count), BF16),
        pltpu.VMEM((1, width), F32),
        pltpu.VMEM((HEAD, width), F32),
    ]


def cost(queries, count):
    return pl.CostEstimate(
        flops=4 * queries * count * HEAD, bytes_accessed=8 * 1024 * 1024, transcendentals=queries * count
    )


def attend_kernel(query_ref, mine_ref, theirs_ref, out_ref, *scratch):
    query, keys, vals, total, accum = scratch
    sources, unused, pixels = mine_ref.shape
    per_step = query_ref.shape[0]
    first = mine_ref.shape[1] - 2 * HEAD

    @pl.when(pl.program_id(0) == 0)
    def _():
        for s in range(sources):
            put_keys(keys, vals, s * pixels, mine_ref[s, first : first + HEAD], mine_ref[s, first + HEAD :])
            put_keys(keys, vals, (sources + s) * pixels, theirs_ref[s, :HEAD], theirs_ref[s, HEAD:])

    query_t = jnp.concatenate([query_ref[s] for s in range(per_step)], axis=1)
    attended = attend_rows(query, keys, vals, total, accum, query_t, 1024)
    for s in range(per_step):
        out_ref[s] = attended[:, s * pixels : (s + 1) * pixels]


def attend(query, mine, theirs):
    sources, unused, pixels = mine.shape
    blocks = query.shape[0]
    per_step = 2
    count = 2 * sources * pixels
    return pl.pallas_call(
        attend_kernel,
        grid=(blocks // per_step,),
        in_specs=[
            pl.BlockSpec((per_step, HEAD, pixels), lambda i: (i, 0, 0)),
            pl.BlockSpec(mine.shape, lambda i: (0, 0, 0)),
            pl.BlockSpec(theirs.shape, lambda i: (0, 0, 0)),
        ],
        out_specs=pl.BlockSpec((per_step, HEAD, pixels), lambda i: (i, 0, 0)),
        out_shape=jax.ShapeDtypeStruct((blocks, HEAD, pixels), BF16),
        scratch_shapes=attention_scratch(count, per_step * pixels),
        compiler_params=pltpu.CompilerParams(vmem_limit_bytes=56 * 2**20),
        cost_estimate=cost(blocks * pixels, count),
    )(query, mine, theirs)


def local(
    features, timestep, w_time, w_emb, b_emb, gn_gain, gn_bias, w_query, w_key, w_value, w_out
):
    unused_one, rows_here, cols_here, channels = features.shape
    pixels = rows_here * cols_here
    per_group = channels // GROUPS
    inner = HEADS * HEAD
    half = half_weights(w_query, w_key, w_value)
    half_theirs = move_col(half, lambda c: c ^ 1)
    weights = gathered_weights(half, half_theirs)

    shift = time_shift(timestep[0], w_time, w_emb, b_emb)
    features, unused = lax.optimization_barrier((features, half_theirs))
    lifted = features.reshape(pixels, channels) + shift
    count = float(pixels * per_group)

    def by_group(value):
        return jnp.sum(jnp.sum(value, axis=0).reshape(GROUPS, per_group), axis=1)

    def by_channel(value):
        return jnp.repeat(value, per_group)[None, :]

    mean_here = by_group(lifted) / count
    spread_here = by_group((lifted - by_channel(mean_here)) ** 2)
    mean, spread = pooled_over_row(jnp.stack([mean_here, spread_here]), count)
    var = spread / (count * lax.axis_size("row"))
    normed = (lifted - by_channel(mean)) / by_channel(jnp.sqrt(var + 1e-06)) * gn_gain + gn_bias
    normed = normed.astype(BF16)

    rows = lax.dot_general(weights, normed, (((1,), (1,)), ((), ())), preferred_element_type=F32)
    rows = rows.astype(BF16).reshape(3, inner, pixels)
    first = CHIPS * HEAD
    by_head = rows[:, :first].reshape(3, CHIPS, HEAD, pixels).transpose(1, 0, 2, 3)
    mine = across_chips(by_head.reshape(CHIPS, 3 * HEAD, pixels))
    theirs = other_core(mine[:, HEAD:])
    upper = lax.axis_index("row") // CHIPS
    rest = rows[:, first:].reshape(3, 2, HEAD, pixels)
    by_head, unused = lax.optimization_barrier((rest[1:].transpose(1, 0, 2, 3), mine))
    by_head = jnp.repeat(by_head.reshape(2, 2 * HEAD, pixels), CHIPS // 2, axis=0)
    pairs = across_chips(by_head)
    pairs_theirs = other_core(pairs)
    opposite = lambda r: (r + 8) % 16
    query = lax.dynamic_index_in_dim(rest[0], upper, 0, keepdims=False)
    query_far = move_row(lax.dynamic_index_in_dim(rest[0], 1 - upper, 0, keepdims=False), opposite)
    core = lax.axis_index("row") % 2
    out_half = lax.dynamic_slice_in_dim(w_out, core * (inner // 2), inner // 2, 0)
    out_half, unused = lax.optimization_barrier((out_half, mine))
    out_half = lax.all_to_all(jnp.broadcast_to(out_half[None], (8,) + out_half.shape), "col", 0, 0, tiled=True)
    out_half = out_half.transpose(1, 0, 2).reshape(inner // 2, channels)
    out_theirs = other_core(out_half)
    out_low = jnp.where(core == 0, out_half, out_theirs)
    out_high = jnp.where(core == 0, out_theirs, out_half)
    full_out = jnp.concatenate([out_low, out_high], axis=0)

    attended = attend(mine, mine, theirs)
    query, attended = lax.optimization_barrier((jnp.stack([query, query_far]), attended))
    attended = across_chips(attended).reshape(first, pixels)
    both = attend(query, pairs, pairs_theirs)
    returned = move_row(both[1], opposite)
    others = jnp.where(upper == 0, jnp.stack([both[0], returned]), jnp.stack([returned, both[0]]))
    attended = jnp.concatenate([attended, others.reshape(inner - first, pixels)], axis=0)
    added = lax.dot_general(attended, full_out, (((0,), (0,)), ((), ())), preferred_element_type=F32)
    return (lifted + added).reshape(1, rows_here, cols_here, channels)


def solution(mesh):
    return jax.shard_map(
        local,
        mesh=mesh,
        in_specs=(
            P("col", "row", None, None),
            P("col"),
            P(),
            P(),
            P(),
            P(),
            P(),
            P("col", None),
            P("col", None),
            P("col", None),
            P(None, "col"),
        ),
        out_specs=P("col", "row", None, None),
        check_vma=False,
    )
```

```python
import functools
import math

import jax
import jax.numpy as jnp
from jax import lax
from jax.experimental import pallas as pl
from jax.experimental.pallas import tpu as pltpu
from jax.sharding import PartitionSpec as P

GROUPS = 32
HEADS = 10
HEAD = 64
CHIPS = 8
F32 = jnp.float32
BF16 = jnp.bfloat16
SCALE = math.log2(math.e) / math.sqrt(HEAD)


def time_shift(step_value, w_time, w_emb, b_emb):
    half = w_time.shape[0] // 2
    freqs = jnp.exp(-math.log(10000.0) * jnp.arange(half, dtype=F32) / half)
    angles = step_value.astype(F32) * freqs
    table = jnp.concatenate([jnp.cos(angles), jnp.sin(angles)])[None, :]
    hidden = jax.nn.silu(jnp.dot(table, w_time, precision=lax.Precision.HIGHEST))
    return jnp.dot(hidden, w_emb, precision=lax.Precision.HIGHEST) + b_emb[None, :]


def move_row(value, target):
    return lax.ppermute(value, "row", [(r, target(r)) for r in range(16)])


def move_col(value, target):
    return lax.ppermute(value, "col", [(c, target(c)) for c in range(8)])


def along_x(step):
    return lambda r: ((r // 4 + step) % 4) * 4 + r % 4


def along_z(step):
    return lambda c: ((c // 2 + step) % 4) * 2 + c % 2


def after(value, *others):
    anywhere = pl.BlockSpec(memory_space=pl.ANY)
    return pl.pallas_call(
        lambda *refs: None,
        in_specs=[anywhere] * (1 + len(others)),
        out_specs=anywhere,
        out_shape=jax.ShapeDtypeStruct(value.shape, value.dtype),
        input_output_aliases={0: 0},
        cost_estimate=pl.CostEstimate(flops=0, bytes_accessed=0, transcendentals=0),
    )(value, *others)


def other_core(value):
    return move_row(value, lambda r: r ^ 1)


def across_chips(value):
    groups = [list(range(0, 16, 2)), list(range(1, 16, 2))]
    return lax.all_to_all(value, "row", 0, 0, tiled=True, axis_index_groups=groups)


def pooled(parts, count):
    mean = sum(p[0] for p in parts) / len(parts)
    spread = sum(p[1] for p in parts) + count * sum((p[0] - mean) ** 2 for p in parts)
    return jnp.stack([mean, spread])


def pooled_over_row(stat, count):
    parts = [stat] + [move_row(stat, along_x(d)) for d in (1, 2, 3)]
    stat = pooled(parts, count)
    parts = [stat] + [move_row(stat, lambda r, k=k: r ^ k) for k in (1, 2, 3)]
    return pooled(parts, 4 * count)


def half_columns_kernel(core_ref, query_ref, key_ref, value_ref, out_w_ref, out_ref, packed):
    def put(low, last, start):
        parts = []
        for ref in (query_ref, key_ref, value_ref):
            parts += [ref[:, low * HEAD : (low + 4) * HEAD], ref[:, last * HEAD : (last + 1) * HEAD]]
        half = out_w_ref.shape[1] // 2
        parts.append(out_w_ref[:, start : start + half])
        packed[...] = jnp.concatenate(parts, axis=1)

    @pl.when(pl.program_id(0) == 0)
    def _():
        @pl.when(core_ref[0] == 0)
        def _():
            put(0, 8, 0)

        @pl.when(core_ref[0] == 1)
        def _():
            put(4, 9, out_w_ref.shape[1] // 2)

    out_ref[0] = packed[...]


def half_columns(w_query, w_key, w_value, w_out):
    core = (lax.axis_index("row") % 2).astype(jnp.int32).reshape(1)
    size = lax.axis_size("col")
    depth = w_query.shape[0]
    width = (3 * w_query.shape[1] + w_out.shape[0]) // 2
    whole = pl.BlockSpec((depth, w_query.shape[1]), lambda i: (0, 0))
    return pl.pallas_call(
        half_columns_kernel,
        grid=(size,),
        in_specs=[pl.BlockSpec(memory_space=pltpu.SMEM)] + [whole] * 4,
        out_specs=pl.BlockSpec((1, depth, width), lambda i: (i, 0, 0)),
        out_shape=jax.ShapeDtypeStruct((size, depth, width), BF16),
        scratch_shapes=[pltpu.VMEM((depth, width), BF16)],
    )(core, w_query, w_key, w_value, w_out.T)


def by_core(mine, theirs):
    core = lax.axis_index("row") % 2
    return jnp.where(core == 0, jnp.stack([mine, theirs]), jnp.stack([theirs, mine]))


def project_kernel(normed_ref, weight_ref, first_ref, last_ref):
    heads = first_ref.shape[0] + 1
    for part in range(3):
        columns = weight_ref[:, :, part * heads * HEAD : (part + 1) * heads * HEAD]
        columns = columns.reshape(normed_ref.shape[1], heads * HEAD)
        out = lax.dot_general(
            normed_ref[...], columns, (((1,), (0,)), ((), ())), preferred_element_type=F32
        )
        out = out.T.astype(BF16)
        for head in range(heads):
            rows = out[head * HEAD : (head + 1) * HEAD]
            if head < heads - 1:
                first_ref[head, part * HEAD : (part + 1) * HEAD, :] = rows
            else:
                last_ref[part * HEAD : (part + 1) * HEAD, :] = rows


def project(normed, weight):
    heads = HEADS // 2
    pixels = normed.shape[0]
    width = -(-3 * heads * HEAD // 128) * 128
    return pl.pallas_call(
        project_kernel,
        grid=(1,),
        in_specs=[
            pl.BlockSpec(normed.shape, lambda i: (0, 0)),
            pl.BlockSpec(weight.shape[:2] + (width,), lambda i: (0, 0, 0)),
        ],
        out_specs=(
            pl.BlockSpec((heads - 1, 3 * HEAD, pixels), lambda i: (0, 0, 0)),
            pl.BlockSpec((3 * HEAD, pixels), lambda i: (0, 0)),
        ),
        out_shape=(
            jax.ShapeDtypeStruct((heads - 1, 3 * HEAD, pixels), BF16),
            jax.ShapeDtypeStruct((3 * HEAD, pixels), BF16),
        ),
        compiler_params=pltpu.CompilerParams(vmem_limit_bytes=48 * 2**20),
        cost_estimate=pl.CostEstimate(
            flops=6 * normed.size * heads * HEAD, bytes_accessed=2**22, transcendentals=0
        ),
    )(normed, weight)


def split3(value):
    high = value.astype(BF16)
    rest = value - high.astype(F32)
    middle = rest.astype(BF16)
    low = (rest - middle.astype(F32)).astype(BF16)
    return high, middle, low


def product(a, b):
    return lax.dot_general(a, b, (((1,), (0,)), ((), ())), preferred_element_type=F32)


def put_keys(keys, vals, place, key_t, value_t):
    count = key_t.shape[1]
    row = lax.broadcasted_iota(jnp.int32, (HEAD, count), 0)
    ones = jnp.where(row < 3, 1.0, 0.0).astype(BF16)
    wide = jnp.concatenate([key_t, key_t, key_t, ones], axis=0)
    keys[place : place + count, :] = wide.T
    vals[:, place : place + count] = value_t


def put_top(query, top):
    width = top.shape[1]
    row = lax.broadcasted_iota(jnp.int32, (HEAD, width), 0)
    high, middle, low = split3(-top)
    wide = [jnp.broadcast_to(part, (HEAD, width)).astype(F32) for part in (high, middle, low)]
    rows = jnp.where(row == 0, wide[0], jnp.where(row == 1, wide[1], jnp.where(row == 2, wide[2], 0.0)))
    query[3 * HEAD :, :] = rows.astype(BF16)


def attend_rows(query, keys, vals, total_ref, accum_ref, query_t, chunk):
    width = query_t.shape[1]
    count = keys.shape[0]
    for at, part in enumerate(split3(query_t.astype(F32) * SCALE)):
        query[at * HEAD : (at + 1) * HEAD, :] = part

    def scores(start, size):
        return product(keys[pl.ds(start, size), :], query[...])

    def run(top, chunk):
        put_top(query, top)

        def step(i, state):
            total, accum = state
            start = pl.multiple_of(i * chunk, chunk)
            weights = jnp.exp2(scores(start, chunk))
            total = total + jnp.sum(weights.reshape(chunk // 8, 8, width), axis=0)
            accum = accum + product(vals[:, pl.ds(start, chunk)], weights.astype(BF16))
            return total, accum

        state = (jnp.zeros((8, width), F32), jnp.zeros((HEAD, width), F32))
        total, accum = lax.fori_loop(0, count // chunk, step, state)
        total_ref[...] = jnp.sum(total, axis=0, keepdims=True)
        accum_ref[...] = accum

    query[3 * HEAD :, :] = jnp.zeros((HEAD, width), BF16)
    run(jnp.max(scores(0, 256), axis=0, keepdims=True), chunk)
    small = jnp.max(jnp.where(total_ref[...] < 1e30, 0.0, 1.0))

    @pl.when(small > 0.5)
    def _():
        query[3 * HEAD :, :] = jnp.zeros((HEAD, width), BF16)

        def step(i, top):
            start = pl.multiple_of(i * 512, 512)
            return jnp.maximum(top, jnp.max(scores(start, 512), axis=0, keepdims=True))

        run(lax.fori_loop(0, count // 512, step, jnp.full((1, width), -jnp.inf, F32)), 512)

    return (accum_ref[...] / total_ref[...]).astype(BF16)


def attention_scratch(count, width):
    return [
        pltpu.VMEM((4 * HEAD, width), BF16),
        pltpu.VMEM((count, 4 * HEAD), BF16),
        pltpu.VMEM((HEAD, count), BF16),
        pltpu.VMEM((1, width), F32),
        pltpu.VMEM((HEAD, width), F32),
    ]


def cost(queries, count):
    return pl.CostEstimate(
        flops=20 * queries * count * HEAD, bytes_accessed=8 * 1024 * 1024, transcendentals=queries * count
    )


def attend_kernel(places_ref, *refs):
    query_refs, (mine_ref, theirs_ref, out_ref), scratch = refs[:2], refs[2:5], refs[5:]
    query, keys, vals, total, accum = scratch
    sources, rows, pixels = mine_ref.shape
    first = rows - 2 * HEAD

    @pl.when(pl.program_id(0) == 0)
    def _():
        for s in range(sources):
            for at, ref in ((s, mine_ref), (sources + s, theirs_ref)):
                put_keys(keys, vals, at * pixels, ref[s, first : first + HEAD], ref[s, first + HEAD :])

    query_t = jnp.concatenate([ref[0] for ref in query_refs], axis=1)
    attended = attend_rows(query, keys, vals, total, accum, query_t, 4096)
    for at in range(2):
        out_ref[at] = attended[:, at * pixels : (at + 1) * pixels]


def attend(places, mine, theirs):
    sources, rows, pixels = mine.shape
    blocks = places.shape[0]
    count = 2 * sources * pixels
    return pl.pallas_call(
        attend_kernel,
        grid_spec=pltpu.PrefetchScalarGridSpec(
            num_scalar_prefetch=1,
            grid=(blocks // 2,),
            in_specs=[
                pl.BlockSpec((1, HEAD, pixels), lambda i, places: (places[2 * i], 0, 0)),
                pl.BlockSpec((1, HEAD, pixels), lambda i, places: (places[2 * i + 1], 0, 0)),
                pl.BlockSpec(mine.shape, lambda i, places: (0, 0, 0)),
                pl.BlockSpec(theirs.shape, lambda i, places: (0, 0, 0)),
            ],
            out_specs=pl.BlockSpec((2, HEAD, pixels), lambda i, places: (i, 0, 0)),
            scratch_shapes=attention_scratch(count, 2 * pixels),
        ),
        out_shape=jax.ShapeDtypeStruct((blocks, HEAD, pixels), BF16),
        compiler_params=pltpu.CompilerParams(vmem_limit_bytes=56 * 2**20),
        cost_estimate=cost(blocks * pixels, count),
    )(places, mine, mine, mine, theirs)


def add_attended_kernel(
    place_ref, features_ref, shift_ref, first_ref, near_ref, far_ref, mine_ref, theirs_ref,
    out_ref, rows, attended, weights,
):
    heads, size, pixels = first_ref.shape
    unused, channels, half = weights.shape
    here = features_ref.shape[2]

    @pl.when(pl.program_id(0) == 0)
    def _():
        upper, core = place_ref[0], place_ref[1]
        rows[: heads * size, :] = first_ref[...].reshape(heads * size, pixels)
        start = heads * size
        rows[pl.ds(pl.multiple_of(start + upper * size, size), size), :] = near_ref[...]
        rows[pl.ds(pl.multiple_of(start + (1 - upper) * size, size), size), :] = far_ref[...]
        for at in range(2):
            attended[at] = rows[at * half : (at + 1) * half, :].T
        weights[core] = mine_ref[:, :, -half:].reshape(channels, half)
        weights[1 - core] = theirs_ref[:, :, -half:].reshape(channels, half)

    here = pl.ds(pl.multiple_of(pl.program_id(0) * here, here), here)
    added = [
        lax.dot_general(
            attended[at, here, :], weights[at], (((1,), (1,)), ((), ())), preferred_element_type=F32
        )
        for at in range(2)
    ]
    out_ref[0, 0] = (features_ref[0, 0] + shift_ref[...]) + (added[0] + added[1])


def add_attended(place, features, shift, first, near, far, mine, theirs):
    unused_one, rows_here, cols_here, channels = features.shape
    pixels = rows_here * cols_here
    half = HEADS * HEAD // 2

    def whole(value):
        return pl.BlockSpec(value.shape, lambda i: (0,) * value.ndim)

    block = pl.BlockSpec((1, 1, cols_here, channels), lambda i: (0, i, 0, 0))
    last = pl.BlockSpec(mine.shape[:2] + (2 * half,), lambda i: (0, 0, mine.shape[2] // (2 * half) - 1))
    return pl.pallas_call(
        add_attended_kernel,
        grid=(rows_here,),
        in_specs=[pl.BlockSpec(memory_space=pltpu.SMEM), block]
        + [whole(value) for value in (shift, first, near, far)]
        + [last, last],
        out_specs=block,
        out_shape=jax.ShapeDtypeStruct(features.shape, F32),
        scratch_shapes=[
            pltpu.VMEM((2 * half, pixels), BF16),
            pltpu.VMEM((2, pixels, half), BF16),
            pltpu.VMEM((2, channels, half), BF16),
        ],
        compiler_params=pltpu.CompilerParams(vmem_limit_bytes=48 * 2**20),
        cost_estimate=pl.CostEstimate(
            flops=4 * features.size * half, bytes_accessed=8 * features.size, transcendentals=0
        ),
    )(place, features, shift, first, near, far, mine, theirs)


def local(
    features, timestep, w_time, w_emb, b_emb, gn_gain, gn_bias, w_query, w_key, w_value, w_out
):
    unused_one, rows_here, cols_here, channels = features.shape
    pixels = rows_here * cols_here
    per_group = channels // GROUPS
    inner = HEADS * HEAD
    mine = half_columns(w_query, w_key, w_value, w_out)
    mine = lax.all_to_all(mine, "col", 0, 0, tiled=True)
    shift = time_shift(timestep[0], w_time, w_emb, b_emb)
    lifted = features.reshape(pixels, channels) + shift
    count = float(pixels * per_group)

    def by_group(value):
        return jnp.sum(jnp.sum(value, axis=0).reshape(GROUPS, per_group), axis=1)

    def by_channel(value):
        return jnp.repeat(value, per_group)[None, :]

    mean_here = by_group(lifted) / count
    spread_here = by_group((lifted - by_channel(mean_here)) ** 2)
    mean, spread = pooled_over_row(jnp.stack([mean_here, spread_here]), count)
    var = spread / (count * lax.axis_size("row"))
    normed = (lifted - by_channel(mean)) / by_channel(jnp.sqrt(var + 1e-06)) * gn_gain + gn_bias
    normed = normed.astype(BF16)

    mine = after(mine, normed)
    theirs = other_core(mine)
    out_weights = (mine, theirs)
    first_mine, last_mine = project(normed, mine)
    first_theirs, last_theirs = project(normed, theirs)
    first = CHIPS * HEAD
    by_head = by_core(first_mine, first_theirs).reshape(CHIPS, 3 * HEAD, pixels)
    mine = across_chips(by_head)
    upper = lax.axis_index("row") // CHIPS
    rest = by_core(last_mine, last_theirs)
    by_head = jnp.repeat(rest, CHIPS // 2, axis=0)
    theirs = other_core(mine)
    pairs = across_chips(after(by_head, mine))

    attended = attend(jnp.arange(CHIPS, dtype=jnp.int32), mine, theirs)
    pairs = after(pairs, attended)
    pairs_theirs = other_core(pairs)
    chip = lax.axis_index("row") // 2
    opposite = lambda r: (r + 8) % 16
    attended = across_chips(attended)
    places = jnp.stack([chip, (chip + 4) % CHIPS]).astype(jnp.int32)
    near, far = attend(places, pairs, pairs_theirs)
    far = move_row(far, opposite)
    place = jnp.stack([upper, lax.axis_index("row") % 2]).astype(jnp.int32)
    return add_attended(place, features, shift, attended, near, far, *out_weights)


def solution(mesh):
    return jax.shard_map(
        local,
        mesh=mesh,
        in_specs=(
            P("col", "row", None, None),
            P("col"),
            P(),
            P(),
            P(),
            P(),
            P(),
            P("col", None),
            P("col", None),
            P("col", None),
            P(None, "col"),
        ),
        out_specs=P("col", "row", None, None),
        check_vma=False,
    )
```

```python
import functools
import math

import jax
import jax.numpy as jnp
from jax import lax
from jax.experimental import pallas as pl
from jax.experimental.pallas import tpu as pltpu
from jax.sharding import PartitionSpec as P

GROUPS = 32
HEADS = 10
HEAD = 64
CHIPS = 8
F32 = jnp.float32
BF16 = jnp.bfloat16
SCALE = math.log2(math.e) / math.sqrt(HEAD)


NO_COST = pl.CostEstimate(flops=0, bytes_accessed=0, transcendentals=0)


def time_shift_kernel(table_ref, time_ref, emb_ref, bias_ref, out_ref, hidden, total):
    step = pl.program_id(0)
    depth = emb_ref.shape[0]

    @pl.when(step == 0)
    def _():
        value = jnp.sum(table_ref[...] * time_ref[...], axis=0, keepdims=True)
        value = value / (1.0 + jnp.exp(-value))
        hidden[...] = jnp.broadcast_to(value, (8, value.shape[1])).T
        total[...] = jnp.zeros_like(total)

    part = hidden[pl.ds(pl.multiple_of(step * depth, depth), depth), 0:1] * emb_ref[...]
    total[...] += jnp.sum(part.reshape(depth // 8, 8, part.shape[1]), axis=0)

    @pl.when(step == pl.num_programs(0) - 1)
    def _():
        out_ref[...] = jnp.sum(total[...], axis=0, keepdims=True) + bias_ref[...]


def time_shift(step_value, w_time, w_emb, b_emb):
    half = w_time.shape[0] // 2
    channels = w_emb.shape[1]
    freqs = jnp.exp(-math.log(10000.0) * jnp.arange(half, dtype=F32) / half)
    angles = step_value.astype(F32) * freqs
    table = jnp.concatenate([jnp.cos(angles), jnp.sin(angles)])[:, None]
    steps = 4
    return pl.pallas_call(
        time_shift_kernel,
        grid=(steps,),
        in_specs=[
            pl.BlockSpec(table.shape, lambda i: (0, 0)),
            pl.BlockSpec(w_time.shape, lambda i: (0, 0)),
            pl.BlockSpec((w_emb.shape[0] // steps, channels), lambda i: (i, 0)),
            pl.BlockSpec((1, channels), lambda i: (0, 0)),
        ],
        out_specs=pl.BlockSpec((1, channels), lambda i: (0, 0)),
        out_shape=jax.ShapeDtypeStruct((1, channels), F32),
        scratch_shapes=[pltpu.VMEM((w_emb.shape[0], 8), F32), pltpu.VMEM((8, channels), F32)],
        compiler_params=pltpu.CompilerParams(vmem_limit_bytes=48 * 2**20),
        cost_estimate=NO_COST,
    )(table, w_time, w_emb, b_emb[None, :])


def spread_kernel(features_ref, out_ref):
    value = features_ref[...].reshape(-1, features_ref.shape[3])
    count = value.shape[0]
    mean = jnp.sum(value, axis=0, keepdims=True) / count
    out_ref[0:1, :] = mean
    out_ref[1:2, :] = jnp.sum((value - mean) ** 2, axis=0, keepdims=True)


def channel_spread(features):
    return pl.pallas_call(
        spread_kernel,
        out_shape=jax.ShapeDtypeStruct((2, features.shape[3]), F32),
        compiler_params=pltpu.CompilerParams(vmem_limit_bytes=48 * 2**20),
        cost_estimate=NO_COST,
    )(features)


def normalise_kernel(features_ref, group_ref, shift_ref, gain_ref, bias_ref, out_ref):
    lifted = features_ref[0, 0] + shift_ref[...]
    value = (lifted - group_ref[0:1, :]) * (1.0 / group_ref[1:2, :])
    out_ref[...] = (value * gain_ref[...] + bias_ref[...]).astype(BF16)


def normalise(features, group, *rows):
    unused, rows_here, cols_here, channels = features.shape
    row = pl.BlockSpec((1, channels), lambda i: (0, 0))
    return pl.pallas_call(
        normalise_kernel,
        grid=(rows_here,),
        in_specs=[
            pl.BlockSpec((1, 1, cols_here, channels), lambda i: (0, i, 0, 0)),
            pl.BlockSpec(group.shape, lambda i: (0, 0)),
        ]
        + [row] * len(rows),
        out_specs=pl.BlockSpec((cols_here, channels), lambda i: (i, 0)),
        out_shape=jax.ShapeDtypeStruct((rows_here * cols_here, channels), BF16),
        cost_estimate=NO_COST,
    )(features, group, *[value.reshape(1, channels) for value in rows])


def move_row(value, target):
    return lax.ppermute(value, "row", [(r, target(r)) for r in range(16)])


def move_col(value, target):
    return lax.ppermute(value, "col", [(c, target(c)) for c in range(8)])


def along_x(step):
    return lambda r: ((r // 4 + step) % 4) * 4 + r % 4


def along_z(step):
    return lambda c: ((c // 2 + step) % 4) * 2 + c % 2


def after(value, *others):
    anywhere = pl.BlockSpec(memory_space=pl.ANY)
    return pl.pallas_call(
        lambda *refs: None,
        in_specs=[anywhere] * (1 + len(others)),
        out_specs=anywhere,
        out_shape=jax.ShapeDtypeStruct(value.shape, value.dtype),
        input_output_aliases={0: 0},
        cost_estimate=pl.CostEstimate(flops=0, bytes_accessed=0, transcendentals=0),
    )(value, *others)


def other_core(value):
    return move_row(value, lambda r: r ^ 1)


def across_chips(value):
    groups = [list(range(0, 16, 2)), list(range(1, 16, 2))]
    return lax.all_to_all(value, "row", 0, 0, tiled=True, axis_index_groups=groups)


def pooled(parts, count):
    mean = sum(p[0] for p in parts) / len(parts)
    spread = sum(p[1] for p in parts) + count * sum((p[0] - mean) ** 2 for p in parts)
    return jnp.stack([mean, spread])


def pooled_over_row(stat, count):
    parts = [stat] + [move_row(stat, along_x(d)) for d in (1, 2, 3)]
    stat = pooled(parts, count)
    parts = [stat] + [move_row(stat, lambda r, k=k: r ^ k) for k in (1, 2, 3)]
    return pooled(parts, 4 * count)


def half_columns_kernel(core_ref, query_ref, key_ref, value_ref, out_w_ref, out_ref, packed, sems):
    def put(low, last, start):
        parts = [out_w_ref[:, start : start + out_w_ref.shape[1] // 2]]
        for head in (low, low + 1, low + 2, low + 3, last):
            parts += [ref[:, head * HEAD : (head + 1) * HEAD] for ref in (query_ref, key_ref, value_ref)]
        packed[...] = jnp.concatenate(parts, axis=1)

    @pl.when(core_ref[0] == 0)
    def _():
        put(0, 8, 0)

    @pl.when(core_ref[0] == 1)
    def _():
        put(4, 9, out_w_ref.shape[1] // 2)

    copies = [pltpu.make_async_copy(packed, out_ref.at[i], sems.at[i]) for i in range(out_ref.shape[0])]
    for copy in copies:
        copy.start()
    for copy in copies:
        copy.wait()


def half_columns(w_query, w_key, w_value, w_out):
    core = (lax.axis_index("row") % 2).astype(jnp.int32).reshape(1)
    size = lax.axis_size("col")
    depth = w_query.shape[0]
    width = (3 * w_query.shape[1] + w_out.shape[0]) // 2
    return pl.pallas_call(
        half_columns_kernel,
        in_specs=[pl.BlockSpec(memory_space=pltpu.SMEM)] + [pl.BlockSpec(memory_space=pltpu.VMEM)] * 4,
        out_specs=pl.BlockSpec(memory_space=pl.ANY),
        out_shape=jax.ShapeDtypeStruct((size, depth, width), BF16),
        scratch_shapes=[pltpu.VMEM((depth, width), BF16), pltpu.SemaphoreType.DMA((size,))],
        compiler_params=pltpu.CompilerParams(vmem_limit_bytes=62 * 2**20),
    )(core, w_query, w_key, w_value, w_out.T)


def by_core(mine, theirs):
    core = lax.axis_index("row") % 2
    return jnp.where(core == 0, jnp.stack([mine, theirs]), jnp.stack([theirs, mine]))


def project_kernel(normed_ref, weight_ref, out_ref):
    weight = weight_ref[...].reshape(normed_ref.shape[1], weight_ref.shape[2])
    out_ref[...] = product(normed_ref[...], weight).T.astype(BF16)


def project(normed, weight):
    pixels, channels = normed.shape
    size, depth, width = weight.shape
    rows = HEADS // 2 * 3 * HEAD
    lanes = 256
    skip = (width - rows) // lanes
    out = pl.pallas_call(
        project_kernel,
        grid=(width // lanes - skip,),
        in_specs=[
            pl.BlockSpec((pixels, channels), lambda i: (0, 0)),
            pl.BlockSpec((size, depth, lanes), lambda i: (0, 0, i + skip)),
        ],
        out_specs=pl.BlockSpec((lanes, pixels), lambda i: (i, 0)),
        out_shape=jax.ShapeDtypeStruct((width - skip * lanes, pixels), BF16),
        compiler_params=pltpu.CompilerParams(vmem_limit_bytes=48 * 2**20),
        cost_estimate=pl.CostEstimate(
            flops=2 * normed.size * rows, bytes_accessed=2**22, transcendentals=0
        ),
    )(normed, weight)
    out = out[-rows:]
    return out[: -3 * HEAD].reshape(HEADS // 2 - 1, 3 * HEAD, pixels), out[-3 * HEAD :]


def split3(value):
    high = value.astype(BF16)
    rest = value - high.astype(F32)
    middle = rest.astype(BF16)
    low = (rest - middle.astype(F32)).astype(BF16)
    return high, middle, low


def product(a, b):
    return lax.dot_general(a, b, (((1,), (0,)), ((), ())), preferred_element_type=F32)


def put_keys(keys, vals, place, key_t, value_t):
    count = key_t.shape[1]
    row = lax.broadcasted_iota(jnp.int32, (HEAD, count), 0)
    ones = jnp.where(row < 3, 1.0, 0.0).astype(BF16)
    wide = jnp.concatenate([key_t, key_t, key_t, ones], axis=0)
    keys[place : place + count, :] = wide.T
    vals[:, place : place + count] = value_t


def put_top(query, top):
    width = top.shape[1]
    row = lax.broadcasted_iota(jnp.int32, (HEAD, width), 0)
    high, middle, low = split3(-top)
    wide = [jnp.broadcast_to(part, (HEAD, width)).astype(F32) for part in (high, middle, low)]
    rows = jnp.where(row == 0, wide[0], jnp.where(row == 1, wide[1], jnp.where(row == 2, wide[2], 0.0)))
    query[3 * HEAD :, :] = rows.astype(BF16)


def attend_rows(query, keys, vals, total_ref, accum_ref, query_t, chunk):
    width = query_t.shape[1]
    count = keys.shape[0]
    for at, part in enumerate(split3(query_t.astype(F32) * SCALE)):
        query[at * HEAD : (at + 1) * HEAD, :] = part

    def scores(start, size):
        return product(keys[pl.ds(start, size), :], query[...])

    def run(top, chunk):
        put_top(query, top)

        def step(i, state):
            total, accum = state
            start = pl.multiple_of(i * chunk, chunk)
            weights = jnp.exp2(scores(start, chunk))
            total = total + jnp.sum(weights.reshape(chunk // 8, 8, width), axis=0)
            accum = accum + product(vals[:, pl.ds(start, chunk)], weights.astype(BF16))
            return total, accum

        state = (jnp.zeros((8, width), F32), jnp.zeros((HEAD, width), F32))
        total, accum = lax.fori_loop(0, count // chunk, step, state)
        total_ref[...] = jnp.sum(total, axis=0, keepdims=True)
        accum_ref[...] = accum

    query[3 * HEAD :, :] = jnp.zeros((HEAD, width), BF16)
    run(jnp.max(scores(0, 256), axis=0, keepdims=True), chunk)
    small = jnp.max(jnp.where(total_ref[...] < 1e30, 0.0, 1.0))

    @pl.when(small > 0.5)
    def _():
        query[3 * HEAD :, :] = jnp.zeros((HEAD, width), BF16)

        def step(i, top):
            start = pl.multiple_of(i * 512, 512)
            return jnp.maximum(top, jnp.max(scores(start, 512), axis=0, keepdims=True))

        run(lax.fori_loop(0, count // 512, step, jnp.full((1, width), -jnp.inf, F32)), 512)

    return (accum_ref[...] / total_ref[...]).astype(BF16)


def attention_scratch(count, width):
    return [
        pltpu.VMEM((4 * HEAD, width), BF16),
        pltpu.VMEM((count, 4 * HEAD), BF16),
        pltpu.VMEM((HEAD, count), BF16),
        pltpu.VMEM((1, width), F32),
        pltpu.VMEM((HEAD, width), F32),
    ]


def cost(queries, count):
    return pl.CostEstimate(
        flops=20 * queries * count * HEAD, bytes_accessed=8 * 1024 * 1024, transcendentals=queries * count
    )


def attend_kernel(stride, query_ref, *refs):
    sources, (out_ref, query, keys, vals, total, accum) = refs[:-6], refs[-6:]
    chips, rows, pixels = sources[0].shape

    @pl.when(pl.program_id(0) == 0)
    def _():
        place = 0
        for ref in sources:
            for chip in range(chips):
                for end in range(stride, rows + 1, stride):
                    key, value = ref[chip, end - 2 * HEAD : end - HEAD], ref[chip, end - HEAD : end]
                    put_keys(keys, vals, place, key, value)
                    place += pixels

    query_t = jnp.concatenate([query_ref[0], query_ref[1]], axis=1)
    attended = attend_rows(query, keys, vals, total, accum, query_t, 8192)
    for at in range(2):
        out_ref[at] = attended[:, at * pixels : (at + 1) * pixels]


def attend(queries, mine, theirs, stride):
    sources = [mine] if theirs is None else [mine, theirs]
    blocks, unused, pixels = queries.shape
    count = sum(source.shape[0] * source.shape[1] // stride * pixels for source in sources)
    return pl.pallas_call(
        functools.partial(attend_kernel, stride),
        grid=(blocks // 2,),
        in_specs=[pl.BlockSpec((2, HEAD, pixels), lambda i: (i, 0, 0))]
        + [pl.BlockSpec(source.shape, lambda i: (0, 0, 0)) for source in sources],
        out_specs=pl.BlockSpec((2, HEAD, pixels), lambda i: (i, 0, 0)),
        out_shape=jax.ShapeDtypeStruct((blocks, HEAD, pixels), BF16),
        scratch_shapes=attention_scratch(count, 2 * pixels),
        compiler_params=pltpu.CompilerParams(vmem_limit_bytes=56 * 2**20),
        cost_estimate=cost(blocks * pixels, count),
    )(queries, *sources)


def add_attended_kernel(
    core_ref, features_ref, shift_ref, first_ref, near_ref, far_ref, mine_ref, theirs_ref,
    out_ref, rows, attended, weights,
):
    heads, size, pixels = first_ref.shape
    unused, channels, half = weights.shape
    here = features_ref.shape[1] * features_ref.shape[2]

    @pl.when(pl.program_id(0) == 0)
    def _():
        core = core_ref[0]
        rows[: heads * size, :] = first_ref[...].reshape(heads * size, pixels)
        start = heads * size
        rows[pl.ds(pl.multiple_of(start + core * size, size), size), :] = near_ref[...]
        rows[pl.ds(pl.multiple_of(start + (1 - core) * size, size), size), :] = far_ref[...]
        for at in range(2):
            attended[at] = rows[at * half : (at + 1) * half, :].T
        weights[core] = mine_ref[:, :, :half].reshape(channels, half)
        weights[1 - core] = theirs_ref[:, :, :half].reshape(channels, half)

    here = pl.ds(pl.multiple_of(pl.program_id(0) * here, here), here)
    added = [
        lax.dot_general(
            attended[at, here, :], weights[at], (((1,), (1,)), ((), ())), preferred_element_type=F32
        )
        for at in range(2)
    ]
    lifted = features_ref[...].reshape(added[0].shape) + shift_ref[...]
    out_ref[...] = (lifted + (added[0] + added[1])).reshape(out_ref.shape)


def add_attended(core, features, shift, first, near, far, mine, theirs):
    unused_one, rows_here, cols_here, channels = features.shape
    pixels = rows_here * cols_here
    half = HEADS * HEAD // 2

    def whole(value):
        return pl.BlockSpec(value.shape, lambda i: (0,) * value.ndim)

    block = pl.BlockSpec((1, rows_here // 2, cols_here, channels), lambda i: (0, i, 0, 0))
    lanes = pl.BlockSpec(mine.shape[:2] + (-(-half // 128) * 128,), lambda i: (0, 0, 0))
    return pl.pallas_call(
        add_attended_kernel,
        grid=(2,),
        in_specs=[pl.BlockSpec(memory_space=pltpu.SMEM), block]
        + [whole(value) for value in (shift, first, near, far)]
        + [lanes, lanes],
        out_specs=block,
        out_shape=jax.ShapeDtypeStruct(features.shape, F32),
        scratch_shapes=[
            pltpu.VMEM((2 * half, pixels), BF16),
            pltpu.VMEM((2, pixels, half), BF16),
            pltpu.VMEM((2, channels, half), BF16),
        ],
        compiler_params=pltpu.CompilerParams(vmem_limit_bytes=48 * 2**20),
        cost_estimate=pl.CostEstimate(
            flops=4 * features.size * half, bytes_accessed=8 * features.size, transcendentals=0
        ),
    )(core, features, shift, first, near, far, mine, theirs)


def local(
    features, timestep, w_time, w_emb, b_emb, gn_gain, gn_bias, w_query, w_key, w_value, w_out
):
    unused_one, rows_here, cols_here, channels = features.shape
    pixels = rows_here * cols_here
    per_group = channels // GROUPS
    inner = HEADS * HEAD
    mine = half_columns(w_query, w_key, w_value, w_out)
    mine = lax.all_to_all(mine, "col", 0, 0, tiled=True)
    pooled_stat = pooled_over_row(channel_spread(features), float(pixels))
    mean, spread = pooled_stat
    shift = time_shift(timestep[0], w_time, w_emb, b_emb)
    count = float(pixels * lax.axis_size("row"))
    means = (mean[None, :] + shift).reshape(GROUPS, per_group)
    mean = jnp.sum(means, axis=1) / per_group
    spread = jnp.sum(spread.reshape(GROUPS, per_group) + count * (means - mean[:, None]) ** 2, axis=1)
    var = spread / (count * per_group)

    group = jnp.repeat(jnp.stack([mean, jnp.sqrt(var + 1e-06)]), per_group, axis=1)
    normed = normalise(features, group, shift, gn_gain, gn_bias)

    mine = after(mine, normed)
    theirs = other_core(mine)
    out_weights = (mine, theirs)
    first_mine, last_mine = project(normed, mine)
    first_theirs, last_theirs = project(normed, theirs)
    first = CHIPS * HEAD
    by_head = by_core(first_mine, first_theirs).reshape(CHIPS, 3 * HEAD, pixels)
    mine = across_chips(by_head)
    rest = jnp.stack([last_mine, other_core(last_theirs)])
    pairs = jnp.broadcast_to(rest[None, :, HEAD:], (CHIPS, 2, 2 * HEAD, pixels))
    theirs = other_core(mine)
    pairs = across_chips(after(pairs, mine))

    attended = attend(mine, mine, theirs, 3 * HEAD)
    pairs = after(pairs, attended)
    attended = across_chips(attended)
    near, far = attend(rest[:, :HEAD], pairs.reshape(CHIPS, 4 * HEAD, pixels), None, 2 * HEAD)
    core = (lax.axis_index("row") % 2).astype(jnp.int32).reshape(1)
    return add_attended(core, features, shift, attended, near, other_core(far), *out_weights)


def solution(mesh):
    return jax.shard_map(
        local,
        mesh=mesh,
        in_specs=(
            P("col", "row", None, None),
            P("col"),
            P(),
            P(),
            P(),
            P(),
            P(),
            P("col", None),
            P("col", None),
            P("col", None),
            P(None, "col"),
        ),
        out_specs=P("col", "row", None, None),
        check_vma=False,
    )
```

```python
import functools
import math

import jax
import jax.numpy as jnp
from jax import lax
from jax.experimental import pallas as pl
from jax.experimental.pallas import tpu as pltpu
from jax.sharding import PartitionSpec as P

GROUPS = 32
HEADS = 10
HEAD = 64
CHIPS = 8
F32 = jnp.float32
BF16 = jnp.bfloat16
SCALE = math.log2(math.e) / math.sqrt(HEAD)


NO_COST = pl.CostEstimate(flops=0, bytes_accessed=0, transcendentals=0)


def time_shift_kernel(table_ref, time_ref, emb_ref, bias_ref, out_ref, hidden, total):
    step = pl.program_id(0)
    depth = emb_ref.shape[0]

    @pl.when(step == 0)
    def _():
        value = jnp.sum(table_ref[...] * time_ref[...], axis=0, keepdims=True)
        value = value / (1.0 + jnp.exp(-value))
        hidden[...] = jnp.broadcast_to(value, (8, value.shape[1])).T
        total[...] = jnp.zeros_like(total)

    part = hidden[pl.ds(pl.multiple_of(step * depth, depth), depth), 0:1] * emb_ref[...]
    total[...] += jnp.sum(part.reshape(depth // 8, 8, part.shape[1]), axis=0)

    @pl.when(step == pl.num_programs(0) - 1)
    def _():
        out_ref[...] = jnp.sum(total[...], axis=0, keepdims=True) + bias_ref[...]


def time_shift(step_value, w_time, w_emb, b_emb):
    half = w_time.shape[0] // 2
    channels = w_emb.shape[1]
    freqs = jnp.exp(-math.log(10000.0) * jnp.arange(half, dtype=F32) / half)
    angles = step_value.astype(F32) * freqs
    table = jnp.concatenate([jnp.cos(angles), jnp.sin(angles)])[:, None]
    steps = 4
    return pl.pallas_call(
        time_shift_kernel,
        grid=(steps,),
        in_specs=[
            pl.BlockSpec(table.shape, lambda i: (0, 0)),
            pl.BlockSpec(w_time.shape, lambda i: (0, 0)),
            pl.BlockSpec((w_emb.shape[0] // steps, channels), lambda i: (i, 0)),
            pl.BlockSpec((1, channels), lambda i: (0, 0)),
        ],
        out_specs=pl.BlockSpec((1, channels), lambda i: (0, 0)),
        out_shape=jax.ShapeDtypeStruct((1, channels), F32),
        scratch_shapes=[pltpu.VMEM((w_emb.shape[0], 8), F32), pltpu.VMEM((8, channels), F32)],
        compiler_params=pltpu.CompilerParams(vmem_limit_bytes=20 * 2**20),
        cost_estimate=NO_COST,
    )(table, w_time, w_emb, b_emb[None, :])


def spread_kernel(features_ref, out_ref):
    value = features_ref[...].reshape(-1, features_ref.shape[3])
    count = value.shape[0]
    mean = jnp.sum(value, axis=0, keepdims=True) / count
    out_ref[0:1, :] = mean
    out_ref[1:2, :] = jnp.sum((value - mean) ** 2, axis=0, keepdims=True)


def channel_spread(features):
    return pl.pallas_call(
        spread_kernel,
        out_shape=jax.ShapeDtypeStruct((2, features.shape[3]), F32),
        compiler_params=pltpu.CompilerParams(vmem_limit_bytes=12 * 2**20),
        cost_estimate=NO_COST,
    )(features)


def normalise_kernel(features_ref, group_ref, shift_ref, gain_ref, bias_ref, out_ref, token_ref):
    lifted = features_ref[0, 0] + shift_ref[...]
    value = (lifted - group_ref[0:1, :]) * (1.0 / group_ref[1:2, :])
    out_ref[...] = (value * gain_ref[...] + bias_ref[...]).astype(BF16)
    token_ref[...] = jnp.broadcast_to(value[:8, :128], token_ref.shape)


def normalise(features, group, *rows):
    unused, rows_here, cols_here, channels = features.shape
    row = pl.BlockSpec((1, channels), lambda i: (0, 0))
    return pl.pallas_call(
        normalise_kernel,
        grid=(rows_here,),
        in_specs=[
            pl.BlockSpec((1, 1, cols_here, channels), lambda i: (0, i, 0, 0)),
            pl.BlockSpec(group.shape, lambda i: (0, 0)),
        ]
        + [row] * len(rows),
        out_specs=(
            pl.BlockSpec((cols_here, channels), lambda i: (i, 0)),
            pl.BlockSpec((8, 128), lambda i: (0, 0)),
        ),
        out_shape=(
            jax.ShapeDtypeStruct((rows_here * cols_here, channels), BF16),
            jax.ShapeDtypeStruct((8, 128), F32),
        ),
        compiler_params=pltpu.CompilerParams(vmem_limit_bytes=8 * 2**20),
        cost_estimate=NO_COST,
    )(features, group, *[value.reshape(1, channels) for value in rows])


def move_row(value, target):
    return lax.ppermute(value, "row", [(r, target(r)) for r in range(16)])


def move_col(value, target):
    return lax.ppermute(value, "col", [(c, target(c)) for c in range(8)])


def along_x(step):
    return lambda r: ((r // 4 + step) % 4) * 4 + r % 4


def along_z(step):
    return lambda c: ((c // 2 + step) % 4) * 2 + c % 2


def after(value, *others, vmem=None):
    anywhere = pl.BlockSpec(memory_space=pl.ANY)
    return pl.pallas_call(
        lambda *refs: None,
        in_specs=[anywhere] * (1 + len(others)),
        out_specs=anywhere,
        out_shape=jax.ShapeDtypeStruct(value.shape, value.dtype),
        input_output_aliases={0: 0},
        compiler_params=pltpu.CompilerParams(vmem_limit_bytes=vmem),
        cost_estimate=pl.CostEstimate(flops=0, bytes_accessed=0, transcendentals=0),
    )(value, *others)


def other_core(value):
    return move_row(value, lambda r: r ^ 1)


def across_chips(value):
    groups = [list(range(0, 16, 2)), list(range(1, 16, 2))]
    return lax.all_to_all(value, "row", 0, 0, tiled=True, axis_index_groups=groups)


def pooled(parts, count):
    mean = sum(p[0] for p in parts) / len(parts)
    spread = sum(p[1] for p in parts) + count * sum((p[0] - mean) ** 2 for p in parts)
    return jnp.stack([mean, spread])


def pooled_over_row(stat, count):
    parts = [stat] + [move_row(stat, along_x(d)) for d in (1, 2, 3)]
    stat = pooled(parts, count)
    parts = [stat] + [move_row(stat, lambda r, k=k: r ^ k) for k in (1, 2, 3)]
    return pooled(parts, 4 * count)


def half_columns_kernel(core_ref, query_ref, key_ref, value_ref, out_w_ref, out_ref, packed, sems):
    def put(low, last, start):
        parts = [out_w_ref[:, start : start + out_w_ref.shape[1] // 2]]
        for head in (low, low + 1, low + 2, low + 3, last):
            parts += [ref[:, head * HEAD : (head + 1) * HEAD] for ref in (query_ref, key_ref, value_ref)]
        packed[...] = jnp.concatenate(parts, axis=1)

    @pl.when(core_ref[0] == 0)
    def _():
        put(0, 8, 0)

    @pl.when(core_ref[0] == 1)
    def _():
        put(4, 9, out_w_ref.shape[1] // 2)

    copies = [pltpu.make_async_copy(packed, out_ref.at[i], sems.at[i]) for i in range(out_ref.shape[0])]
    for copy in copies:
        copy.start()
    for copy in copies:
        copy.wait()


def half_columns(w_query, w_key, w_value, w_out):
    core = (lax.axis_index("row") % 2).astype(jnp.int32).reshape(1)
    size = lax.axis_size("col")
    depth = w_query.shape[0]
    width = (3 * w_query.shape[1] + w_out.shape[0]) // 2
    return pl.pallas_call(
        half_columns_kernel,
        in_specs=[pl.BlockSpec(memory_space=pltpu.SMEM)] + [pl.BlockSpec(memory_space=pltpu.VMEM)] * 4,
        out_specs=pl.BlockSpec(memory_space=pl.ANY),
        out_shape=jax.ShapeDtypeStruct((size, depth, width), BF16),
        scratch_shapes=[pltpu.VMEM((depth, width), BF16), pltpu.SemaphoreType.DMA((size,))],
        compiler_params=pltpu.CompilerParams(vmem_limit_bytes=62 * 2**20),
    )(core, w_query, w_key, w_value, w_out.T)


def by_core(mine, theirs):
    core = lax.axis_index("row") % 2
    return jnp.where(core == 0, jnp.stack([mine, theirs]), jnp.stack([theirs, mine]))


def project_kernel(normed_ref, weight_ref, out_ref, last_ref):
    weight = weight_ref[...].reshape(normed_ref.shape[1], weight_ref.shape[2])
    out = product(normed_ref[...], weight).T.astype(BF16)
    out_ref[...] = out

    @pl.when(pl.program_id(0) == pl.num_programs(0) - 1)
    def _():
        last_ref[...] = out[-last_ref.shape[0] :]


def project(normed, weight):
    pixels, channels = normed.shape
    size, depth, width = weight.shape
    rows = HEADS // 2 * 3 * HEAD
    last = 3 * HEAD
    lanes = 256
    skip = (width - rows) // lanes
    out, last_out = pl.pallas_call(
        project_kernel,
        grid=(width // lanes - skip,),
        in_specs=[
            pl.BlockSpec((pixels, channels), lambda i: (0, 0)),
            pl.BlockSpec((size, depth, lanes), lambda i: (0, 0, i + skip)),
        ],
        out_specs=(
            pl.BlockSpec((lanes, pixels), lambda i: (i, 0)),
            pl.BlockSpec((last, pixels), lambda i: (0, 0)),
        ),
        out_shape=(
            jax.ShapeDtypeStruct((width - skip * lanes, pixels), BF16),
            jax.ShapeDtypeStruct((last, pixels), BF16),
        ),
        compiler_params=pltpu.CompilerParams(vmem_limit_bytes=16 * 2**20),
        cost_estimate=pl.CostEstimate(
            flops=2 * normed.size * rows, bytes_accessed=2**22, transcendentals=0
        ),
    )(normed, weight)
    return out[-rows:-last].reshape(HEADS // 2 - 1, last, pixels), last_out


def split3(value):
    high = value.astype(BF16)
    rest = value - high.astype(F32)
    middle = rest.astype(BF16)
    low = (rest - middle.astype(F32)).astype(BF16)
    return high, middle, low


def product(a, b):
    return lax.dot_general(a, b, (((1,), (0,)), ((), ())), preferred_element_type=F32)


def put_keys(keys, vals, place, key_t, value_t):
    count = key_t.shape[1]
    row = lax.broadcasted_iota(jnp.int32, (HEAD, count), 0)
    ones = jnp.where(row < 3, 1.0, 0.0).astype(BF16)
    wide = jnp.concatenate([key_t, key_t, key_t, ones], axis=0)
    keys[place : place + count, :] = wide.T
    vals[:, place : place + count] = value_t


def put_top(query, top):
    width = top.shape[1]
    row = lax.broadcasted_iota(jnp.int32, (HEAD, width), 0)
    high, middle, low = split3(-top)
    wide = [jnp.broadcast_to(part, (HEAD, width)).astype(F32) for part in (high, middle, low)]
    rows = jnp.where(row == 0, wide[0], jnp.where(row == 1, wide[1], jnp.where(row == 2, wide[2], 0.0)))
    query[3 * HEAD :, :] = rows.astype(BF16)


def attend_rows(query, keys, vals, total_ref, accum_ref, query_t, chunk):
    width = query_t.shape[1]
    count = keys.shape[0]
    for at, part in enumerate(split3(query_t.astype(F32) * SCALE)):
        query[at * HEAD : (at + 1) * HEAD, :] = part

    def scores(start, size):
        return product(keys[pl.ds(start, size), :], query[...])

    def run(top, chunk):
        put_top(query, top)

        def step(i, state):
            total, accum = state
            start = pl.multiple_of(i * chunk, chunk)
            weights = jnp.exp2(scores(start, chunk))
            total = total + jnp.sum(weights.reshape(chunk // 8, 8, width), axis=0)
            accum = accum + product(vals[:, pl.ds(start, chunk)], weights.astype(BF16))
            return total, accum

        state = (jnp.zeros((8, width), F32), jnp.zeros((HEAD, width), F32))
        total, accum = lax.fori_loop(0, count // chunk, step, state)
        total_ref[...] = jnp.sum(total, axis=0, keepdims=True)
        accum_ref[...] = accum

    query[3 * HEAD :, :] = jnp.zeros((HEAD, width), BF16)
    run(jnp.max(scores(0, 128), axis=0, keepdims=True), chunk)
    small = jnp.max(jnp.where(total_ref[...] < 1e30, 0.0, 1.0))

    @pl.when(small > 0.5)
    def _():
        query[3 * HEAD :, :] = jnp.zeros((HEAD, width), BF16)

        def step(i, top):
            start = pl.multiple_of(i * 512, 512)
            return jnp.maximum(top, jnp.max(scores(start, 512), axis=0, keepdims=True))

        run(lax.fori_loop(0, count // 512, step, jnp.full((1, width), -jnp.inf, F32)), 512)

    return (accum_ref[...] / total_ref[...]).astype(BF16)


def attention_scratch(count, width):
    return [
        pltpu.VMEM((4 * HEAD, width), BF16),
        pltpu.VMEM((count, 4 * HEAD), BF16),
        pltpu.VMEM((HEAD, count), BF16),
        pltpu.VMEM((1, width), F32),
        pltpu.VMEM((HEAD, width), F32),
    ]


def cost(queries, count):
    return pl.CostEstimate(
        flops=20 * queries * count * HEAD, bytes_accessed=8 * 1024 * 1024, transcendentals=queries * count
    )


def attend_kernel(stride, split, query_low, query_high, *refs):
    ends = 7 if split else 6
    sources, outs, (query, keys, vals, total, accum) = refs[:-ends], refs[-ends:-5], refs[-5:]
    chips, rows, pixels = sources[0].shape

    @pl.when(pl.program_id(0) == 0)
    def _():
        place = 0
        for ref in sources:
            for chip in range(chips):
                for end in range(stride, rows + 1, stride):
                    key, value = ref[chip, end - 2 * HEAD : end - HEAD], ref[chip, end - HEAD : end]
                    put_keys(keys, vals, place, key, value)
                    place += pixels

    if split:
        query_t = jnp.concatenate([query_low[:HEAD], query_high[:HEAD]], axis=1)
    else:
        query_t = jnp.concatenate([query_low[0], query_high[0]], axis=1)
    attended = attend_rows(query, keys, vals, total, accum, query_t, keys.shape[0])
    for at in range(2):
        value = attended[:, at * pixels : (at + 1) * pixels]
        if split:
            outs[at][...] = value
        else:
            outs[0][at] = value


def attend(low, high, mine, theirs, stride):
    sources = [mine] if theirs is None else [mine, theirs]
    split = low.ndim == 2
    pixels = low.shape[-1]
    count = sum(source.shape[0] * source.shape[1] // stride * pixels for source in sources)
    if split:
        blocks = 2
        queries = [pl.BlockSpec((HEAD, pixels), lambda i: (0, 0))] * 2
        out_specs = [pl.BlockSpec((HEAD, pixels), lambda i: (0, 0))] * 2
        out_shape = [jax.ShapeDtypeStruct((HEAD, pixels), BF16)] * 2
    else:
        blocks = low.shape[0]
        queries = [pl.BlockSpec((1, HEAD, pixels), lambda i, at=at: (2 * i + at, 0, 0)) for at in range(2)]
        out_specs = pl.BlockSpec((2, HEAD, pixels), lambda i: (i, 0, 0))
        out_shape = jax.ShapeDtypeStruct((blocks, HEAD, pixels), BF16)
    return pl.pallas_call(
        functools.partial(attend_kernel, stride, split),
        grid=(blocks // 2,),
        in_specs=queries + [pl.BlockSpec(source.shape, lambda i: (0, 0, 0)) for source in sources],
        out_specs=out_specs,
        out_shape=out_shape,
        scratch_shapes=attention_scratch(count, 2 * pixels),
        compiler_params=pltpu.CompilerParams(vmem_limit_bytes=56 * 2**20),
        cost_estimate=cost(blocks * pixels, count),
    )(low, high, *sources)


def add_attended_kernel(
    core_ref, features_ref, shift_ref, first_ref, near_ref, far_ref, mine_ref, theirs_ref,
    out_ref, rows, attended, weights,
):
    heads, size, pixels = first_ref.shape
    unused, channels, half = weights.shape
    here = features_ref.shape[1] * features_ref.shape[2]

    @pl.when(pl.program_id(0) == 0)
    def _():
        core = core_ref[0]
        rows[: heads * size, :] = first_ref[...].reshape(heads * size, pixels)
        start = heads * size
        rows[pl.ds(pl.multiple_of(start + core * size, size), size), :] = near_ref[...]
        rows[pl.ds(pl.multiple_of(start + (1 - core) * size, size), size), :] = far_ref[...]
        for at in range(2):
            attended[at] = rows[at * half : (at + 1) * half, :].T
        weights[core] = mine_ref[:, :, :half].reshape(channels, half)
        weights[1 - core] = theirs_ref[:, :, :half].reshape(channels, half)

    here = pl.ds(pl.multiple_of(pl.program_id(0) * here, here), here)
    added = [
        lax.dot_general(
            attended[at, here, :], weights[at], (((1,), (1,)), ((), ())), preferred_element_type=F32
        )
        for at in range(2)
    ]
    lifted = features_ref[...].reshape(added[0].shape) + shift_ref[...]
    out_ref[...] = (lifted + (added[0] + added[1])).reshape(out_ref.shape)


def add_attended(core, features, shift, first, near, far, mine, theirs):
    unused_one, rows_here, cols_here, channels = features.shape
    pixels = rows_here * cols_here
    half = HEADS * HEAD // 2

    def whole(value):
        return pl.BlockSpec(value.shape, lambda i: (0,) * value.ndim)

    block = pl.BlockSpec((1, rows_here // 2, cols_here, channels), lambda i: (0, i, 0, 0))
    lanes = pl.BlockSpec(mine.shape[:2] + (-(-half // 128) * 128,), lambda i: (0, 0, 0))
    return pl.pallas_call(
        add_attended_kernel,
        grid=(2,),
        in_specs=[pl.BlockSpec(memory_space=pltpu.SMEM), block]
        + [whole(value) for value in (shift, first, near, far)]
        + [lanes, lanes],
        out_specs=block,
        out_shape=jax.ShapeDtypeStruct(features.shape, F32),
        scratch_shapes=[
            pltpu.VMEM((2 * half, pixels), BF16),
            pltpu.VMEM((2, pixels, half), BF16),
            pltpu.VMEM((2, channels, half), BF16),
        ],
        compiler_params=pltpu.CompilerParams(vmem_limit_bytes=48 * 2**20),
        cost_estimate=pl.CostEstimate(
            flops=4 * features.size * half, bytes_accessed=8 * features.size, transcendentals=0
        ),
    )(core, features, shift, first, near, far, mine, theirs)


def local(
    features, timestep, w_time, w_emb, b_emb, gn_gain, gn_bias, w_query, w_key, w_value, w_out
):
    unused_one, rows_here, cols_here, channels = features.shape
    pixels = rows_here * cols_here
    per_group = channels // GROUPS
    inner = HEADS * HEAD
    mine = half_columns(w_query, w_key, w_value, w_out)
    mine = lax.all_to_all(mine, "col", 0, 0, tiled=True)
    pooled_stat = pooled_over_row(channel_spread(features), float(pixels))
    mean, spread = pooled_stat
    shift = time_shift(timestep[0], w_time, w_emb, b_emb)
    count = float(pixels * lax.axis_size("row"))
    means = (mean[None, :] + shift).reshape(GROUPS, per_group)
    mean = jnp.sum(means, axis=1) / per_group
    spread = jnp.sum(spread.reshape(GROUPS, per_group) + count * (means - mean[:, None]) ** 2, axis=1)
    var = spread / (count * per_group)

    group = jnp.repeat(jnp.stack([mean, jnp.sqrt(var + 1e-06)]), per_group, axis=1)
    normed, done = normalise(features, group, shift, gn_gain, gn_bias)

    mine = after(mine, done, vmem=2**20)
    theirs = other_core(mine)
    out_weights = (mine, theirs)
    first_mine, last_mine = project(normed, mine)
    first_theirs, last_theirs = project(normed, theirs)
    first = CHIPS * HEAD
    by_head = by_core(first_mine, first_theirs).reshape(CHIPS, 3 * HEAD, pixels)
    mine = across_chips(by_head)
    last_theirs = other_core(last_theirs)
    pairs = jnp.concatenate([last_mine[HEAD:], last_theirs[HEAD:]], axis=0)
    pairs = jnp.broadcast_to(pairs[None], (CHIPS,) + pairs.shape)
    theirs = other_core(mine)
    pairs = across_chips(after(pairs, mine))

    attended = attend(mine, mine, mine, theirs, 3 * HEAD)
    pairs = after(pairs, attended)
    attended = across_chips(attended)
    near, far = attend(last_mine, last_theirs, pairs, None, 2 * HEAD)
    core = (lax.axis_index("row") % 2).astype(jnp.int32).reshape(1)
    return add_attended(core, features, shift, attended, near, other_core(far), *out_weights)


def solution(mesh):
    return jax.shard_map(
        local,
        mesh=mesh,
        in_specs=(
            P("col", "row", None, None),
            P("col"),
            P(),
            P(),
            P(),
            P(),
            P(),
            P("col", None),
            P("col", None),
            P("col", None),
            P(None, "col"),
        ),
        out_specs=P("col", "row", None, None),
        check_vma=False,
    )
```

```python
import functools
import math

import jax
import jax.numpy as jnp
from jax import lax
from jax.experimental import pallas as pl
from jax.experimental.pallas import tpu as pltpu
from jax.sharding import PartitionSpec as P

GROUPS = 32
HEADS = 10
HEAD = 64
CHIPS = 8
F32 = jnp.float32
BF16 = jnp.bfloat16
SCALE = math.log2(math.e) / math.sqrt(HEAD)


NO_COST = pl.CostEstimate(flops=0, bytes_accessed=0, transcendentals=0)


def time_shift_kernel(table_ref, time_ref, emb_ref, bias_ref, out_ref, hidden, total):
    step = pl.program_id(0)
    depth = emb_ref.shape[0]

    @pl.when(step == 0)
    def _():
        value = jnp.sum(table_ref[...] * time_ref[...], axis=0, keepdims=True)
        value = value / (1.0 + jnp.exp(-value))
        hidden[...] = jnp.broadcast_to(value, (8, value.shape[1])).T
        total[...] = jnp.zeros_like(total)

    part = hidden[pl.ds(pl.multiple_of(step * depth, depth), depth), 0:1] * emb_ref[...]
    total[...] += jnp.sum(part.reshape(depth // 8, 8, part.shape[1]), axis=0)

    @pl.when(step == pl.num_programs(0) - 1)
    def _():
        out_ref[...] = jnp.sum(total[...], axis=0, keepdims=True) + bias_ref[...]


def time_shift(step_value, w_time, w_emb, b_emb):
    half = w_time.shape[0] // 2
    channels = w_emb.shape[1]
    freqs = jnp.exp(-math.log(10000.0) * jnp.arange(half, dtype=F32) / half)
    angles = step_value.astype(F32) * freqs
    table = jnp.concatenate([jnp.cos(angles), jnp.sin(angles)])[:, None]
    steps = 4
    return pl.pallas_call(
        time_shift_kernel,
        grid=(steps,),
        in_specs=[
            pl.BlockSpec(table.shape, lambda i: (0, 0)),
            pl.BlockSpec(w_time.shape, lambda i: (0, 0)),
            pl.BlockSpec((w_emb.shape[0] // steps, channels), lambda i: (i, 0)),
            pl.BlockSpec((1, channels), lambda i: (0, 0)),
        ],
        out_specs=pl.BlockSpec((1, channels), lambda i: (0, 0)),
        out_shape=jax.ShapeDtypeStruct((1, channels), F32),
        scratch_shapes=[pltpu.VMEM((w_emb.shape[0], 8), F32), pltpu.VMEM((8, channels), F32)],
        compiler_params=pltpu.CompilerParams(vmem_limit_bytes=20 * 2**20),
        cost_estimate=NO_COST,
    )(table, w_time, w_emb, b_emb[None, :])


def spread_kernel(features_ref, out_ref):
    value = features_ref[...].reshape(-1, features_ref.shape[3])
    count = value.shape[0]
    mean = jnp.sum(value, axis=0, keepdims=True) / count
    out_ref[0:1, :] = mean
    out_ref[1:2, :] = jnp.sum((value - mean) ** 2, axis=0, keepdims=True)


def channel_spread(features):
    return pl.pallas_call(
        spread_kernel,
        out_shape=jax.ShapeDtypeStruct((2, features.shape[3]), F32),
        compiler_params=pltpu.CompilerParams(vmem_limit_bytes=12 * 2**20),
        cost_estimate=NO_COST,
    )(features)


def normalise_kernel(features_ref, group_ref, shift_ref, gain_ref, bias_ref, out_ref, token_ref):
    lifted = features_ref[0, 0] + shift_ref[...]
    value = (lifted - group_ref[0:1, :]) * (1.0 / group_ref[1:2, :])
    out_ref[...] = (value * gain_ref[...] + bias_ref[...]).astype(BF16)
    token_ref[...] = jnp.broadcast_to(value[:8, :128], token_ref.shape)


def normalise(features, group, *rows):
    unused, rows_here, cols_here, channels = features.shape
    row = pl.BlockSpec((1, channels), lambda i: (0, 0))
    return pl.pallas_call(
        normalise_kernel,
        grid=(rows_here,),
        in_specs=[
            pl.BlockSpec((1, 1, cols_here, channels), lambda i: (0, i, 0, 0)),
            pl.BlockSpec(group.shape, lambda i: (0, 0)),
        ]
        + [row] * len(rows),
        out_specs=(
            pl.BlockSpec((cols_here, channels), lambda i: (i, 0)),
            pl.BlockSpec((8, 128), lambda i: (0, 0)),
        ),
        out_shape=(
            jax.ShapeDtypeStruct((rows_here * cols_here, channels), BF16),
            jax.ShapeDtypeStruct((8, 128), F32),
        ),
        compiler_params=pltpu.CompilerParams(vmem_limit_bytes=8 * 2**20),
        cost_estimate=NO_COST,
    )(features, group, *[value.reshape(1, channels) for value in rows])


def move_row(value, target):
    return lax.ppermute(value, "row", [(r, target(r)) for r in range(16)])


def move_col(value, target):
    return lax.ppermute(value, "col", [(c, target(c)) for c in range(8)])


def along_x(step):
    return lambda r: ((r // 4 + step) % 4) * 4 + r % 4


def along_z(step):
    return lambda c: ((c // 2 + step) % 4) * 2 + c % 2


def after(value, *others, vmem=None):
    anywhere = pl.BlockSpec(memory_space=pl.ANY)
    return pl.pallas_call(
        lambda *refs: None,
        in_specs=[anywhere] * (1 + len(others)),
        out_specs=anywhere,
        out_shape=jax.ShapeDtypeStruct(value.shape, value.dtype),
        input_output_aliases={0: 0},
        compiler_params=pltpu.CompilerParams(vmem_limit_bytes=vmem),
        cost_estimate=pl.CostEstimate(flops=0, bytes_accessed=0, transcendentals=0),
    )(value, *others)


def other_core(value):
    return move_row(value, lambda r: r ^ 1)


def across_chips(value):
    groups = [list(range(0, 16, 2)), list(range(1, 16, 2))]
    return lax.all_to_all(value, "row", 0, 0, tiled=True, axis_index_groups=groups)


def pooled(parts, count):
    mean = sum(p[0] for p in parts) / len(parts)
    spread = sum(p[1] for p in parts) + count * sum((p[0] - mean) ** 2 for p in parts)
    return jnp.stack([mean, spread])


def pooled_over_row(stat, count):
    parts = [stat] + [move_row(stat, along_x(d)) for d in (1, 2, 3)]
    stat = pooled(parts, count)
    parts = [stat] + [move_row(stat, lambda r, k=k: r ^ k) for k in (1, 2, 3)]
    return pooled(parts, 4 * count)


def half_columns_kernel(core_ref, query_ref, key_ref, value_ref, out_w_ref, out_ref, packed, sems):
    def put(low, last, start):
        parts = [out_w_ref[:, start : start + out_w_ref.shape[1] // 2]]
        for head in (low, low + 1, low + 2, low + 3, last):
            parts += [ref[:, head * HEAD : (head + 1) * HEAD] for ref in (query_ref, key_ref, value_ref)]
        packed[...] = jnp.concatenate(parts, axis=1)

    @pl.when(core_ref[0] == 0)
    def _():
        put(0, 8, 0)

    @pl.when(core_ref[0] == 1)
    def _():
        put(4, 9, out_w_ref.shape[1] // 2)

    copies = [pltpu.make_async_copy(packed, out_ref.at[i], sems.at[i]) for i in range(out_ref.shape[0])]
    for copy in copies:
        copy.start()
    for copy in copies:
        copy.wait()


def half_columns(w_query, w_key, w_value, w_out):
    core = (lax.axis_index("row") % 2).astype(jnp.int32).reshape(1)
    size = lax.axis_size("col")
    depth = w_query.shape[0]
    width = (3 * w_query.shape[1] + w_out.shape[0]) // 2
    return pl.pallas_call(
        half_columns_kernel,
        in_specs=[pl.BlockSpec(memory_space=pltpu.SMEM)] + [pl.BlockSpec(memory_space=pltpu.VMEM)] * 4,
        out_specs=pl.BlockSpec(memory_space=pl.ANY),
        out_shape=jax.ShapeDtypeStruct((size, depth, width), BF16),
        scratch_shapes=[pltpu.VMEM((depth, width), BF16), pltpu.SemaphoreType.DMA((size,))],
        compiler_params=pltpu.CompilerParams(vmem_limit_bytes=62 * 2**20),
    )(core, w_query, w_key, w_value, w_out.T)


def by_core(mine, theirs):
    core = lax.axis_index("row") % 2
    return jnp.where(core == 0, jnp.stack([mine, theirs]), jnp.stack([theirs, mine]))


def project_kernel(normed_ref, weight_ref, out_ref, last_ref):
    weight = weight_ref[...].reshape(normed_ref.shape[1], weight_ref.shape[2])
    out = product(normed_ref[...], weight).T.astype(BF16)
    out_ref[...] = out

    @pl.when(pl.program_id(0) == pl.num_programs(0) - 1)
    def _():
        last_ref[...] = out[-last_ref.shape[0] :]


def project(normed, weight):
    pixels, channels = normed.shape
    size, depth, width = weight.shape
    rows = HEADS // 2 * 3 * HEAD
    last = 3 * HEAD
    lanes = 256
    skip = (width - rows) // lanes
    out, last_out = pl.pallas_call(
        project_kernel,
        grid=(width // lanes - skip,),
        in_specs=[
            pl.BlockSpec((pixels, channels), lambda i: (0, 0)),
            pl.BlockSpec((size, depth, lanes), lambda i: (0, 0, i + skip)),
        ],
        out_specs=(
            pl.BlockSpec((lanes, pixels), lambda i: (i, 0)),
            pl.BlockSpec((last, pixels), lambda i: (0, 0)),
        ),
        out_shape=(
            jax.ShapeDtypeStruct((width - skip * lanes, pixels), BF16),
            jax.ShapeDtypeStruct((last, pixels), BF16),
        ),
        compiler_params=pltpu.CompilerParams(vmem_limit_bytes=16 * 2**20),
        cost_estimate=pl.CostEstimate(
            flops=2 * normed.size * rows, bytes_accessed=2**22, transcendentals=0
        ),
    )(normed, weight)
    return out[-rows:-last].reshape(HEADS // 2 - 1, last, pixels), last_out


def split3(value):
    high = value.astype(BF16)
    rest = value - high.astype(F32)
    middle = rest.astype(BF16)
    low = (rest - middle.astype(F32)).astype(BF16)
    return high, middle, low


def product(a, b):
    return lax.dot_general(a, b, (((1,), (0,)), ((), ())), preferred_element_type=F32)


def put_keys(keys, vals, place, key_t, value_t):
    count = key_t.shape[1]
    row = lax.broadcasted_iota(jnp.int32, (HEAD, count), 0)
    ones = jnp.where(row < 3, 1.0, 0.0).astype(BF16)
    wide = jnp.concatenate([key_t, key_t, key_t, ones], axis=0)
    keys[place : place + count, :] = wide.T
    vals[:, place : place + count] = value_t


def put_top(query, top):
    width = top.shape[1]
    row = lax.broadcasted_iota(jnp.int32, (HEAD, width), 0)
    high, middle, low = split3(-top)
    wide = [jnp.broadcast_to(part, (HEAD, width)).astype(F32) for part in (high, middle, low)]
    rows = jnp.where(row == 0, wide[0], jnp.where(row == 1, wide[1], jnp.where(row == 2, wide[2], 0.0)))
    query[3 * HEAD :, :] = rows.astype(BF16)


def attend_rows(query, keys, vals, total_ref, accum_ref, query_t, chunk):
    width = query_t.shape[1]
    count = keys.shape[0]
    for at, part in enumerate(split3(query_t.astype(F32) * SCALE)):
        query[at * HEAD : (at + 1) * HEAD, :] = part

    def scores(start, size):
        return product(keys[pl.ds(start, size), :], query[...])

    def run(top, chunk):
        put_top(query, top)

        def step(i, state):
            total, accum = state
            start = pl.multiple_of(i * chunk, chunk)
            weights = jnp.exp2(scores(start, chunk))
            total = total + jnp.sum(weights.reshape(chunk // 8, 8, width), axis=0)
            accum = accum + product(vals[:, pl.ds(start, chunk)], weights.astype(BF16))
            return total, accum

        state = (jnp.zeros((8, width), F32), jnp.zeros((HEAD, width), F32))
        total, accum = lax.fori_loop(0, count // chunk, step, state)
        total_ref[...] = jnp.sum(total, axis=0, keepdims=True)
        accum_ref[...] = accum

    query[3 * HEAD :, :] = jnp.zeros((HEAD, width), BF16)
    run(jnp.max(scores(0, 128), axis=0, keepdims=True), chunk)
    small = jnp.max(jnp.where(total_ref[...] < 1e30, 0.0, 1.0))

    @pl.when(small > 0.5)
    def _():
        query[3 * HEAD :, :] = jnp.zeros((HEAD, width), BF16)

        def step(i, top):
            start = pl.multiple_of(i * 512, 512)
            return jnp.maximum(top, jnp.max(scores(start, 512), axis=0, keepdims=True))

        run(lax.fori_loop(0, count // 512, step, jnp.full((1, width), -jnp.inf, F32)), 512)

    return (accum_ref[...] / total_ref[...]).astype(BF16)


def attention_scratch(count, width):
    return [
        pltpu.VMEM((4 * HEAD, width), BF16),
        pltpu.VMEM((count, 4 * HEAD), BF16),
        pltpu.VMEM((HEAD, count), BF16),
        pltpu.VMEM((1, width), F32),
        pltpu.VMEM((HEAD, width), F32),
    ]


def cost(queries, count):
    return pl.CostEstimate(
        flops=20 * queries * count * HEAD, bytes_accessed=8 * 1024 * 1024, transcendentals=queries * count
    )


def attend_kernel(stride, split, query_low, query_high, *refs):
    ends = 7 if split else 6
    sources, outs, (query, keys, vals, total, accum) = refs[:-ends], refs[-ends:-5], refs[-5:]
    chips, rows, pixels = sources[0].shape

    @pl.when(pl.program_id(0) == 0)
    def _():
        place = 0
        for ref in sources:
            for chip in range(chips):
                for end in range(stride, rows + 1, stride):
                    key, value = ref[chip, end - 2 * HEAD : end - HEAD], ref[chip, end - HEAD : end]
                    put_keys(keys, vals, place, key, value)
                    place += pixels

    if split:
        query_t = jnp.concatenate([query_low[:HEAD], query_high[:HEAD]], axis=1)
    else:
        query_t = jnp.concatenate([query_low[0], query_high[0]], axis=1)
    attended = attend_rows(query, keys, vals, total, accum, query_t, keys.shape[0])
    for at in range(2):
        value = attended[:, at * pixels : (at + 1) * pixels]
        if split:
            outs[at][...] = value
        else:
            outs[0][at] = value


def attend(low, high, mine, theirs, stride):
    sources = [mine] if theirs is None else [mine, theirs]
    split = low.ndim == 2
    pixels = low.shape[-1]
    count = sum(source.shape[0] * source.shape[1] // stride * pixels for source in sources)
    if split:
        blocks = 2
        queries = [pl.BlockSpec((HEAD, pixels), lambda i: (0, 0))] * 2
        out_specs = [pl.BlockSpec((HEAD, pixels), lambda i: (0, 0))] * 2
        out_shape = [jax.ShapeDtypeStruct((HEAD, pixels), BF16)] * 2
    else:
        blocks = low.shape[0]
        queries = [pl.BlockSpec((1, HEAD, pixels), lambda i, at=at: (2 * i + at, 0, 0)) for at in range(2)]
        out_specs = pl.BlockSpec((2, HEAD, pixels), lambda i: (i, 0, 0))
        out_shape = jax.ShapeDtypeStruct((blocks, HEAD, pixels), BF16)
    return pl.pallas_call(
        functools.partial(attend_kernel, stride, split),
        grid=(blocks // 2,),
        in_specs=queries + [pl.BlockSpec(source.shape, lambda i: (0, 0, 0)) for source in sources],
        out_specs=out_specs,
        out_shape=out_shape,
        scratch_shapes=attention_scratch(count, 2 * pixels),
        compiler_params=pltpu.CompilerParams(vmem_limit_bytes=56 * 2**20),
        cost_estimate=cost(blocks * pixels, count),
    )(low, high, *sources)


def add_attended_kernel(
    core_ref, features_ref, shift_ref, first_ref, near_ref, far_ref, mine_ref, theirs_ref,
    out_ref, rows, attended, weights,
):
    heads, size, pixels = first_ref.shape
    unused, channels, half = weights.shape
    here = features_ref.shape[1] * features_ref.shape[2]

    @pl.when(pl.program_id(0) == 0)
    def _():
        core = core_ref[0]
        rows[: heads * size, :] = first_ref[...].reshape(heads * size, pixels)
        start = heads * size
        rows[pl.ds(pl.multiple_of(start + core * size, size), size), :] = near_ref[...]
        rows[pl.ds(pl.multiple_of(start + (1 - core) * size, size), size), :] = far_ref[...]
        for at in range(2):
            attended[at] = rows[at * half : (at + 1) * half, :].T
        weights[core] = mine_ref[:, :, :half].reshape(channels, half)
        weights[1 - core] = theirs_ref[:, :, :half].reshape(channels, half)

    here = pl.ds(pl.multiple_of(pl.program_id(0) * here, here), here)
    added = [
        lax.dot_general(
            attended[at, here, :], weights[at], (((1,), (1,)), ((), ())), preferred_element_type=F32
        )
        for at in range(2)
    ]
    lifted = features_ref[...].reshape(added[0].shape) + shift_ref[...]
    out_ref[...] = (lifted + (added[0] + added[1])).reshape(out_ref.shape)


def add_attended(core, features, shift, first, near, far, mine, theirs):
    unused_one, rows_here, cols_here, channels = features.shape
    pixels = rows_here * cols_here
    half = HEADS * HEAD // 2

    def whole(value):
        return pl.BlockSpec(value.shape, lambda i: (0,) * value.ndim)

    block = pl.BlockSpec((1, rows_here // 2, cols_here, channels), lambda i: (0, i, 0, 0))
    lanes = pl.BlockSpec(mine.shape[:2] + (-(-half // 128) * 128,), lambda i: (0, 0, 0))
    return pl.pallas_call(
        add_attended_kernel,
        grid=(2,),
        in_specs=[pl.BlockSpec(memory_space=pltpu.SMEM), block]
        + [whole(value) for value in (shift, first, near, far)]
        + [lanes, lanes],
        out_specs=block,
        out_shape=jax.ShapeDtypeStruct(features.shape, F32),
        scratch_shapes=[
            pltpu.VMEM((2 * half, pixels), BF16),
            pltpu.VMEM((2, pixels, half), BF16),
            pltpu.VMEM((2, channels, half), BF16),
        ],
        compiler_params=pltpu.CompilerParams(vmem_limit_bytes=48 * 2**20),
        cost_estimate=pl.CostEstimate(
            flops=4 * features.size * half, bytes_accessed=8 * features.size, transcendentals=0
        ),
    )(core, features, shift, first, near, far, mine, theirs)


def local(
    features, timestep, w_time, w_emb, b_emb, gn_gain, gn_bias, w_query, w_key, w_value, w_out
):
    unused_one, rows_here, cols_here, channels = features.shape
    pixels = rows_here * cols_here
    per_group = channels // GROUPS
    inner = HEADS * HEAD
    mine = half_columns(w_query, w_key, w_value, w_out)
    mine = lax.all_to_all(mine, "col", 0, 0, tiled=True)
    pooled_stat = pooled_over_row(channel_spread(features), float(pixels))
    mean, spread = pooled_stat
    shift = time_shift(timestep[0], w_time, w_emb, b_emb)
    count = float(pixels * lax.axis_size("row"))
    means = (mean[None, :] + shift).reshape(GROUPS, per_group)
    mean = jnp.sum(means, axis=1) / per_group
    spread = jnp.sum(spread.reshape(GROUPS, per_group) + count * (means - mean[:, None]) ** 2, axis=1)
    var = spread / (count * per_group)

    group = jnp.repeat(jnp.stack([mean, jnp.sqrt(var + 1e-06)]), per_group, axis=1)
    normed, done = normalise(features, group, shift, gn_gain, gn_bias)

    mine = after(mine, group, shift, vmem=2**20)
    theirs = other_core(mine)
    out_weights = (mine, theirs)
    first_mine, last_mine = project(normed, mine)
    first_theirs, last_theirs = project(normed, theirs)
    first = CHIPS * HEAD
    by_head = by_core(first_mine, first_theirs).reshape(CHIPS, 3 * HEAD, pixels)
    mine = across_chips(by_head)
    last_theirs = other_core(last_theirs)
    pairs = jnp.concatenate([last_mine[HEAD:], last_theirs[HEAD:]], axis=0)
    pairs = jnp.broadcast_to(pairs[None], (CHIPS,) + pairs.shape)
    theirs = other_core(mine)
    pairs = across_chips(after(pairs, mine))

    attended = attend(mine, mine, mine, theirs, 3 * HEAD)
    pairs = after(pairs, attended)
    attended = across_chips(attended)
    near, far = attend(last_mine, last_theirs, pairs, None, 2 * HEAD)
    core = (lax.axis_index("row") % 2).astype(jnp.int32).reshape(1)
    return add_attended(core, features, shift, attended, near, other_core(far), *out_weights)


def solution(mesh):
    return jax.shard_map(
        local,
        mesh=mesh,
        in_specs=(
            P("col", "row", None, None),
            P("col"),
            P(),
            P(),
            P(),
            P(),
            P(),
            P("col", None),
            P("col", None),
            P("col", None),
            P(None, "col"),
        ),
        out_specs=P("col", "row", None, None),
        check_vma=False,
    )
```
